32 devices in a mesh: gx: 8 (over z, y), gy: 4 (over x, core).
Axes of the slice: x: 2, y: 2, z: 4, core: 2. Of those that a mesh axis runs over, the one named last changes fastest.
Arguments:
- features: bfloat16 [32, 16, 512, 128], P('gx', 'gy'), may hold values from -6 to 6
- occupancy: int32 [32, 16], P('gx', 'gy'), may hold values from 0 to 1, as said below
- pair_offset: int32 [32, 16, 9], P('gx', 'gy'), may hold values from 0 to 27, as said below
- owner: int32 [32, 16], P('gx', 'gy'), may hold values from 0 to 7, as said below
- w_sub: bfloat16 [27, 128, 128], replicated, may hold values from -0.25 to 0.25
- w_down: bfloat16 [1024, 256], replicated, may hold values from -0.1875 to 0.1875
- cotangent: bfloat16 [32, 16, 64, 256], P('gx', 'gy'), may hold values from -6 to 6
Outputs:
- coarse: bfloat16 [32, 16, 64, 256], P('gx', 'gy')
- feature_grad: bfloat16 [32, 16, 512, 128], P('gx', 'gy')
- sub_grad: float32 [27, 128, 128], replicated
- down_grad: float32 [1024, 256], replicated
The draws below stay inside these ranges and needn't reach their ends.
Inputs may be any that keep to these rules, and one draw needn't show every extreme that they name: `occupancy`: 1 where a column holds an occupied brick. `pair_offset`: entry k = 3 (dx + 1) + (dy + 1) of a column is 9 (dx + 1) + 3 (dy + 1) + (dz + 1) when that column and the neighbour column at dx, dy are both inside the grid and occupied and the neighbour's brick lies dz in -1..1 levels higher, else 27. The relation is symmetric: the neighbour's entry back is 27 exactly when this one is, and otherwise the two sum to 26. A column's coarse cell lies on device (owner, same gy index), at the same place within that device's 4 x 4 block as the column has in its own block. (owner minus the column's own gx index) modulo 8 depends only on the gy index and the place, so each device holds exactly one cell per place; each device sends exactly 2 columns to each device of its gx row, itself included.
All inputs are finite; a program needn't handle non-finite values.
Results may differ from the reference program's by a relative error of at most 0.005.
Values may be sent and summed in bfloat16 or wider, within the bound.
A program may use at most 192 MiB of HBM per device.

```python
import jax
import jax.numpy as jnp
from jax import lax

FINE_CHANNELS = 128
COARSE_CHANNELS2 = 256
E = 8
LOCAL_BRICKS_X = 4
LOCAL_BRICKS_Y = 4
PX = 8
PY = 4
GLOBAL_BRICKS_X = 32
GLOBAL_BRICKS_Y = 16
NB = 16
BRICK_VOXELS = 512
COARSE_PER_BRICK = 64
NDEV = 32


NEIGHBOURS = [(-1, -1), (-1, 0), (-1, 1), (0, -1), (0, 0), (0, 1), (1, -1), (1, 0), (1, 1)]


def ground(key):
    column_heights = jax.random.randint(jax.random.fold_in(key, 11), (GLOBAL_BRICKS_X, GLOBAL_BRICKS_Y), 0, 4)
    brick_present = (jax.random.randint(jax.random.fold_in(key, 12), (GLOBAL_BRICKS_X, GLOBAL_BRICKS_Y), 0, 4) > 0).astype(jnp.int32)
    return (column_heights, brick_present)


def draw_occupancy(key, part):
    column_heights, brick_present = ground(key)
    key = jax.random.fold_in(key, 1)
    return brick_present.astype(jnp.int32)


def draw_pair_offset(key, part):
    column_heights, brick_present = ground(key)
    key = jax.random.fold_in(key, 2)
    height_padded = jnp.pad(column_heights, 1)
    present_padded = jnp.pad(brick_present, 1)
    columns = []
    for direction, (stepping_x, stepping_y) in enumerate(NEIGHBOURS):
        nearby_height = height_padded[1 + stepping_x:1 + stepping_x + GLOBAL_BRICKS_X, 1 + stepping_y:1 + stepping_y + GLOBAL_BRICKS_Y]
        nearby_present = present_padded[1 + stepping_x:1 + stepping_x + GLOBAL_BRICKS_X, 1 + stepping_y:1 + stepping_y + GLOBAL_BRICKS_Y]
        height_step = nearby_height - column_heights
        linked = (brick_present * nearby_present > 0) & (jnp.abs(height_step) <= 1)
        columns.append(jnp.where(linked, 3 * direction + height_step + 1, 27))
    return jnp.stack(columns, -1).astype(jnp.int32)


def draw_owner(key, part):
    key = jax.random.fold_in(key, 3)
    shift_pool = jnp.tile(jnp.arange(PX, dtype=jnp.int32), NB // PX)
    shifts = jax.vmap(lambda group: jax.random.permutation(jax.random.fold_in(key, group), shift_pool))(jnp.arange(PY))
    column_holder = jnp.arange(GLOBAL_BRICKS_X, dtype=jnp.int32) // LOCAL_BRICKS_X
    placement_index = (jnp.arange(GLOBAL_BRICKS_X, dtype=jnp.int32) % LOCAL_BRICKS_X)[:, None] * LOCAL_BRICKS_Y + (jnp.arange(GLOBAL_BRICKS_Y, dtype=jnp.int32) % LOCAL_BRICKS_Y)[None, :]
    row_grouping = jnp.broadcast_to((jnp.arange(GLOBAL_BRICKS_Y, dtype=jnp.int32) // LOCAL_BRICKS_Y)[None, :], (GLOBAL_BRICKS_X, GLOBAL_BRICKS_Y))
    shift_value = shifts[row_grouping, placement_index]
    return ((column_holder[:, None] + shift_value) % PX).astype(jnp.int32)


def levels(key, dims, shards, low, top_value):
    factor_of, own = 1.0, jax.random.fold_in(key, 6)
    for dim, shards_of in shards:
        steps = jnp.exp(jax.random.uniform(jax.random.fold_in(own, dim), (shards_of,), jnp.float32, low / len(shards), top_value / len(shards)))
        factor_of = factor_of * jnp.repeat(steps, dims[dim] // shards_of).reshape([-1 if axis == dim else 1 for axis in range(len(dims))])
    return factor_of


def noise(rng, dims, scale, most, split=(), kind=jnp.bfloat16):
    values = jax.random.normal(rng, dims, jnp.float32) * scale
    if len(split) > 0:
        values = levels(rng, dims, split, -0.22, 0.18) * values
    return jnp.clip(values, min=-most, max=most).astype(kind)


def setup_inputs(seed: int = 0) -> dict:
    key_of = jax.random.split(jax.random.key(seed), 8)
    return {
        "features": noise(key_of[0], (GLOBAL_BRICKS_X, GLOBAL_BRICKS_Y, BRICK_VOXELS, FINE_CHANNELS), 1.0, 6.0, ((0, 8), (1, 4))),
        "occupancy": draw_occupancy(jax.random.fold_in(key_of[7], 71), 0),
        "pair_offset": draw_pair_offset(jax.random.fold_in(key_of[7], 71), 0),
        "owner": draw_owner(jax.random.fold_in(key_of[7], 71), 0),
        "w_sub": noise(key_of[4], (27, FINE_CHANNELS, FINE_CHANNELS), (4 * FINE_CHANNELS) ** -0.5, 0.25),
        "w_down": noise(key_of[5], (8 * FINE_CHANNELS, COARSE_CHANNELS2), (8 * FINE_CHANNELS) ** -0.5, 0.1875),
        "cotangent": noise(key_of[6], (GLOBAL_BRICKS_X, GLOBAL_BRICKS_Y, COARSE_PER_BRICK, COARSE_CHANNELS2), 1.0, 6.0, ((0, 8), (1, 4))),
    }


NEIGHBOURS = [(-1, -1), (-1, 0), (-1, 1), (0, -1), (0, 0), (0, 1), (1, -1), (1, 0), (1, 1)]


def bricks_to_patches(values):
    leading = values.shape[:-2]
    channels = values.shape[-1]
    half_edge = E // 2
    depth = len(leading)
    blocks = values.reshape(leading + (half_edge, 2, half_edge, 2, half_edge, 2, channels))
    layout = tuple(range(depth)) + (depth, depth + 2, depth + 4, depth + 1, depth + 3, depth + 5, depth + 6)
    return blocks.transpose(layout).reshape(leading + (half_edge ** 3, 8 * channels))


def patches_to_bricks(values, channels):
    leading = values.shape[:-2]
    half_edge = E // 2
    depth = len(leading)
    blocks = values.reshape(leading + (half_edge, half_edge, half_edge, 2, 2, 2, channels))
    layout = tuple(range(depth)) + (depth, depth + 3, depth + 1, depth + 4, depth + 2, depth + 5, depth + 6)
    return blocks.transpose(layout).reshape(leading + (E ** 3, channels))


def reference(features, occupancy, pair_offset, owner, w_sub, w_down, cotangent):
    brick_present = occupancy.astype(jnp.float32)[:, :, None, None]
    masked = features * occupancy.astype(jnp.bfloat16)[:, :, None, None]
    weight_table = jnp.concatenate([w_sub, jnp.zeros((1, FINE_CHANNELS, FINE_CHANNELS), jnp.bfloat16)], 0).astype(jnp.float32)
    padded = jnp.pad(masked, ((1, 1), (1, 1), (0, 0), (0, 0)))
    mirrored = jnp.where(pair_offset == 27, 27, 26 - pair_offset).astype(jnp.int32)
    row_identifiers = jnp.arange(GLOBAL_BRICKS_X, dtype=jnp.int32)
    codes = jnp.arange(28, dtype=jnp.int32)

    def conv_row(row):
        window = lax.dynamic_slice_in_dim(padded, row, 3, 0).astype(jnp.float32)
        offsets = lax.dynamic_index_in_dim(pair_offset, row, 0, keepdims=False)
        total = jnp.zeros((GLOBAL_BRICKS_Y, BRICK_VOXELS, FINE_CHANNELS), jnp.float32)
        for direction, (stepping_x, stepping_y) in enumerate(NEIGHBOURS):
            source = window[1 + stepping_x, 1 + stepping_y:1 + stepping_y + GLOBAL_BRICKS_Y]
            chosen = weight_table[offsets[:, direction]]
            total = total + jnp.einsum("bvc,bcd->bvd", source, chosen)
        return total

    preact = lax.map(conv_row, row_identifiers)
    sigmoid_pre = jax.nn.sigmoid(preact)
    hidden_features = (brick_present * (masked.astype(jnp.float32) + preact * sigmoid_pre)).astype(jnp.bfloat16)
    brick_patches = bricks_to_patches(hidden_features).reshape(GLOBAL_BRICKS_X * GLOBAL_BRICKS_Y * COARSE_PER_BRICK, 8 * FINE_CHANNELS)
    shifted_rows = jnp.dot(brick_patches, w_down, preferred_element_type=jnp.float32).astype(jnp.bfloat16)
    shifted_rows = shifted_rows.reshape(GLOBAL_BRICKS_X, GLOBAL_BRICKS_Y, COARSE_PER_BRICK, COARSE_CHANNELS2)
    destination_x = (owner * LOCAL_BRICKS_X + (jnp.arange(GLOBAL_BRICKS_X, dtype=jnp.int32) % LOCAL_BRICKS_X)[:, None]).astype(jnp.int32)
    destination_y = jnp.broadcast_to(jnp.arange(GLOBAL_BRICKS_Y, dtype=jnp.int32)[None, :], (GLOBAL_BRICKS_X, GLOBAL_BRICKS_Y))
    coarse = jnp.zeros((GLOBAL_BRICKS_X, GLOBAL_BRICKS_Y, COARSE_PER_BRICK, COARSE_CHANNELS2), jnp.bfloat16).at[destination_x, destination_y].set(shifted_rows)
    returned_rows = cotangent[destination_x, destination_y].reshape(GLOBAL_BRICKS_X * GLOBAL_BRICKS_Y * COARSE_PER_BRICK, COARSE_CHANNELS2)
    down_grad = lax.dot_general(brick_patches, returned_rows, (((0,), (0,)), ((), ())), preferred_element_type=jnp.float32) / NDEV
    patch_gradient = lax.dot_general(returned_rows, w_down, (((1,), (1,)), ((), ())), preferred_element_type=jnp.float32)
    hidden_gradient = patches_to_bricks(patch_gradient.reshape(GLOBAL_BRICKS_X, GLOBAL_BRICKS_Y, COARSE_PER_BRICK, 8 * FINE_CHANNELS), FINE_CHANNELS)
    slope_value = sigmoid_pre * (1.0 + preact * (1.0 - sigmoid_pre))
    pre_grad = (brick_present * hidden_gradient * slope_value).astype(jnp.bfloat16)
    padded_grad = jnp.pad(pre_grad, ((1, 1), (1, 1), (0, 0), (0, 0)))

    def back_row(row):
        window = lax.dynamic_slice_in_dim(padded, row, 3, 0).astype(jnp.float32)
        grad_window = lax.dynamic_slice_in_dim(padded_grad, row, 3, 0).astype(jnp.float32)
        offsets = lax.dynamic_index_in_dim(pair_offset, row, 0, keepdims=False)
        mirror_row = lax.dynamic_index_in_dim(mirrored, row, 0, keepdims=False)
        own_grad = grad_window[1, 1:1 + GLOBAL_BRICKS_Y]
        conv_total = jnp.zeros((GLOBAL_BRICKS_Y, BRICK_VOXELS, FINE_CHANNELS), jnp.float32)
        sub_total = jnp.zeros((28, FINE_CHANNELS, FINE_CHANNELS), jnp.float32)
        for direction, (stepping_x, stepping_y) in enumerate(NEIGHBOURS):
            source = window[1 + stepping_x, 1 + stepping_y:1 + stepping_y + GLOBAL_BRICKS_Y]
            outer = jnp.einsum("bvc,bvd->bcd", source, own_grad, precision=lax.Precision.HIGHEST)
            selector = (offsets[:, direction][:, None] == codes[None, :]).astype(jnp.float32)
            sub_total = sub_total + jnp.einsum("bo,bcd->ocd", selector, outer, precision=lax.Precision.HIGHEST)
            chosen = weight_table[mirror_row[:, direction]]
            neighbour_grad = grad_window[1 + stepping_x, 1 + stepping_y:1 + stepping_y + GLOBAL_BRICKS_Y]
            conv_total = conv_total + jnp.einsum("bvd,bcd->bvc", neighbour_grad, chosen)
        return conv_total, sub_total

    conv_grad, sub_rows = lax.map(back_row, row_identifiers)
    feature_grad = (brick_present * (hidden_gradient + conv_grad)).astype(jnp.bfloat16)
    sub_grad = jnp.sum(sub_rows, 0)[:27] / NDEV
    return coarse, feature_grad, sub_grad, down_grad
```

```python
import functools

import jax
import jax.numpy as jnp
from jax import lax
from jax.experimental import pallas as pl
from jax.experimental.pallas import tpu as pltpu
from jax.sharding import PartitionSpec as P

MESH = pl.DeviceIdType.MESH
E = 8
NEIGHBOURS = [(-1, -1), (-1, 0), (-1, 1), (0, -1), (0, 0), (0, 1), (1, -1), (1, 0), (1, 1)]
HALO = [k for k in range(9) if k != 4]
F32 = jnp.float32
BF16 = jnp.bfloat16
VMEM_LIMIT = 52 * 1024 * 1024


def position():
    return lax.axis_index("gx"), lax.axis_index("gy")


def exists(nx, ny, gx, gy, k):
    dx, dy = NEIGHBOURS[k]
    x, y = gx + dx, gy + dy
    return (x >= 0) & (x < nx) & (y >= 0) & (y < ny)


def edge(ref, width_x, width_y, k):
    dx, dy = NEIGHBOURS[k]
    sx = {-1: 0, 0: slice(None), 1: width_x - 1}[dx]
    sy = {-1: 0, 0: slice(None), 1: width_y - 1}[dy]
    return ref.at[sx, sy]


def slot(halo, k):
    hx, hy, hc = halo
    dx, dy = NEIGHBOURS[k]
    if dy == 0:
        return hx.at[(dx + 1) // 2]
    if dx == 0:
        return hy.at[(dy + 1) // 2]
    return hc.at[(dx + 1) // 2 * 2 + (dy + 1) // 2]


def halo_copy(nx, ny, gx, gy, source, halo, send, recv, k):
    dx, dy = NEIGHBOURS[k]
    return pltpu.make_async_remote_copy(
        src_ref=edge(source, source.shape[0], source.shape[1], k),
        dst_ref=slot(halo, 8 - k),
        send_sem=send.at[k],
        recv_sem=recv.at[8 - k],
        device_id=(gx + dx, gy + dy),
        device_id_type=MESH,
    )


def halo_arrival(nx, ny, gx, gy, source, halo, send, recv, k):
    dx, dy = NEIGHBOURS[k]
    return pltpu.make_async_remote_copy(
        src_ref=edge(source, source.shape[0], source.shape[1], 8 - k),
        dst_ref=slot(halo, k),
        send_sem=send.at[8 - k],
        recv_sem=recv.at[k],
        device_id=(gx + dx, gy + dy),
        device_id_type=MESH,
    )


def halo_fill(source, halo, recv, k):
    return pltpu.make_async_copy(
        edge(source, source.shape[0], source.shape[1], k), slot(halo, k), recv.at[k]
    )


def start_halo(nx, ny, gx, gy, source, halo, send, recv):
    for k in HALO:
        there = exists(nx, ny, gx, gy, k)

        @pl.when(there)
        def _(k=k):
            halo_copy(nx, ny, gx, gy, source, halo, send, recv, k).start()

        @pl.when(jnp.logical_not(there))
        def _(k=k):
            halo_fill(source, halo, recv, k).start()


def finish_halo(nx, ny, gx, gy, source, halo, send, recv):
    for k in HALO:
        there = exists(nx, ny, gx, gy, k)

        @pl.when(there)
        def _(k=k):
            halo_copy(nx, ny, gx, gy, source, halo, send, recv, k).wait_send()
            halo_arrival(nx, ny, gx, gy, source, halo, send, recv, k).wait_recv()

        @pl.when(jnp.logical_not(there))
        def _(k=k):
            halo_fill(source, halo, recv, k).wait()


def exchange_copy(nx, gx, gy, outgoing, incoming, send, recv, shift):
    peer = lax.rem(gx + shift, nx)
    return pltpu.make_async_remote_copy(
        src_ref=outgoing.at[peer],
        dst_ref=incoming.at[gx],
        send_sem=send.at[shift],
        recv_sem=recv.at[shift],
        device_id=(peer, gy),
        device_id_type=MESH,
    )


def exchange_arrival(nx, gx, gy, outgoing, incoming, send, recv, shift):
    peer = lax.rem(gx + nx - shift, nx)
    return pltpu.make_async_remote_copy(
        src_ref=outgoing.at[peer],
        dst_ref=incoming.at[peer],
        send_sem=send.at[shift],
        recv_sem=recv.at[shift],
        device_id=(peer, gy),
        device_id_type=MESH,
    )


def start_exchange(nx, gx, gy, outgoing, incoming, send, recv):
    pltpu.make_async_copy(outgoing.at[gx], incoming.at[gx], recv.at[0]).start()
    for shift in range(1, nx):
        exchange_copy(nx, gx, gy, outgoing, incoming, send, recv, shift).start()


def finish_exchange(nx, gx, gy, outgoing, incoming, send, recv):
    pltpu.make_async_copy(outgoing.at[gx], incoming.at[gx], recv.at[0]).wait()
    for shift in range(1, nx):
        exchange_copy(nx, gx, gy, outgoing, incoming, send, recv, shift).wait_send()
        exchange_arrival(nx, gx, gy, outgoing, incoming, send, recv, shift).wait_recv()


def greet(nx, ny, gx, gy, partners):
    barrier = pltpu.get_barrier_semaphore()
    for k in HALO:
        dx, dy = NEIGHBOURS[k]

        @pl.when(exists(nx, ny, gx, gy, k))
        def _(dx=dx, dy=dy):
            pl.semaphore_signal(
                barrier, inc=1, device_id=(gx + dx, gy + dy), device_id_type=MESH
            )

    for shift in range(1, nx):
        pl.semaphore_signal(
            barrier, inc=1, device_id=(lax.rem(gx + shift, nx), gy), device_id_type=MESH
        )
    for partner in partners:
        pl.semaphore_signal(barrier, inc=1, device_id=partner, device_id_type=MESH)
    count = nx - 1 + len(partners)
    for k in HALO:
        count = count + jnp.where(exists(nx, ny, gx, gy, k), 1, 0)
    pl.semaphore_wait(barrier, count)


def open_kernel(nx, ny, order, features, cotangent, hx, hy, hc, incoming, outgoing, hs, hr, es, er):
    gx, gy = position()
    halo = (hx, hy, hc)
    greet(nx, ny, gx, gy, [])
    start_halo(nx, ny, gx, gy, features, halo, hs, hr)
    share = outgoing.shape[1]
    for peer in range(nx):
        for i in range(share):
            outgoing[peer, i] = cotangent[order[peer * share + i]]
    start_exchange(nx, gx, gy, outgoing, incoming, es, er)
    finish_exchange(nx, gx, gy, outgoing, incoming, es, er)
    finish_halo(nx, ny, gx, gy, features, halo, hs, hr)


def groups(nx, ny):
    deep = 4 if nx % 4 == 0 else 1
    return [
        (axis, stride, size)
        for axis, stride, size in (
            (1, 1, 2),
            (1, 2, ny // 2),
            (0, 1, nx // deep),
            (0, nx // deep, deep),
        )
        if size > 1
    ]


def member(gx, gy, group, shift):
    axis, stride, size = group
    here = (gx, gy)[axis]
    own = lax.rem(lax.div(here, stride), size)
    other = lax.rem(own + shift, size)
    there = here + (other - own) * stride
    return own, other, ((there, gy) if axis == 0 else (gx, there))


def reduce_all(nx, ny, gx, gy, partial, total, sends, recvs, ss, rs, gs, gr):
    rows = partial.shape[0]
    plan = groups(nx, ny)
    base, length = 0, rows
    bases = []
    sem = 0
    for stage, group in enumerate(plan):
        size = group[2]
        chunk = length // size
        copies = []
        own = None
        for shift in range(1, size):
            own, other, device = member(gx, gy, group, shift)
            start = pl.multiple_of(base + other * chunk, 16)
            sends[stage][shift - 1] = partial[pl.ds(start, chunk)].astype(BF16)
            copy = pltpu.make_async_remote_copy(
                src_ref=sends[stage].at[shift - 1],
                dst_ref=recvs[stage].at[shift - 1],
                send_sem=ss.at[sem],
                recv_sem=rs.at[sem],
                device_id=device,
                device_id_type=MESH,
            )
            copy.start()
            copies.append(copy)
            sem += 1
        bases.append(base)
        base = pl.multiple_of(base + own * chunk, 16)
        length = chunk
        for copy in copies:
            copy.wait()
        value = partial[pl.ds(base, chunk)]
        for shift in range(1, size):
            value = value + recvs[stage][shift - 1].astype(F32)
        partial[pl.ds(base, chunk)] = value
    total[pl.ds(base, length)] = (partial[pl.ds(base, length)]).astype(BF16)
    sem = 0
    for stage in reversed(range(len(plan))):
        group = plan[stage]
        size = group[2]
        copies = []
        for shift in range(1, size):
            own, other, device = member(gx, gy, group, shift)
            back = lax.rem(own + size - shift, size)
            copies.append(
                (
                    pltpu.make_async_remote_copy(
                        src_ref=total.at[pl.ds(base, length)],
                        dst_ref=total.at[pl.ds(base, length)],
                        send_sem=gs.at[sem],
                        recv_sem=gr.at[sem],
                        device_id=device,
                        device_id_type=MESH,
                    ),
                    pl.multiple_of(bases[stage] + back * length, 16),
                    sem,
                    device,
                )
            )
            copies[-1][0].start()
            sem += 1
        for copy, start, index, device in copies:
            copy.wait_send()
            pltpu.make_async_remote_copy(
                src_ref=total.at[pl.ds(base, length)],
                dst_ref=total.at[pl.ds(start, length)],
                send_sem=gs.at[index],
                recv_sem=gr.at[index],
                device_id=device,
                device_id_type=MESH,
            ).wait_recv()
        base = bases[stage]
        length = length * size


def close_kernel(
    nx, ny, stages, pre_grad, outgoing, partial_in, hx, hy, hc, incoming, result, *scratch
):
    sends, recvs = scratch[:stages], scratch[stages : 2 * stages]
    partial, total, hs, hr, es, er, ss, rs, gs, gr, ls = scratch[2 * stages :]
    gx, gy = position()
    halo = (hx, hy, hc)
    load = pltpu.make_async_copy(partial_in, partial, ls)
    load.start()
    plan = groups(nx, ny)
    partners = [
        member(gx, gy, group, shift)[2] for group in plan for shift in range(1, group[2])
    ]
    greet(nx, ny, gx, gy, partners)
    start_halo(nx, ny, gx, gy, pre_grad, halo, hs, hr)
    start_exchange(nx, gx, gy, outgoing, incoming, es, er)
    load.wait()
    reduce_all(nx, ny, gx, gy, partial, total, sends, recvs, ss, rs, gs, gr)
    result[...] = total[...]
    finish_exchange(nx, gx, gy, outgoing, incoming, es, er)
    finish_halo(nx, ny, gx, gy, pre_grad, halo, hs, hr)


def ext_source(width_x, width_y, refs, x, y):
    own, hx, hy, hc = refs
    sx = 0 if x < 0 else (2 if x >= width_x else 1)
    sy = 0 if y < 0 else (2 if y >= width_y else 1)
    if sx == 1 and sy == 1:
        return own, (x, y)
    if sy == 1:
        return hx, (sx // 2, y)
    if sx == 1:
        return hy, (sy // 2, x)
    return hc, (sx // 2 * 2 + sy // 2,)


def voxel_order(transposed):
    row = lax.broadcasted_iota(jnp.int32, (E**3, E**3), 1 if transposed else 0)
    column = lax.broadcasted_iota(jnp.int32, (E**3, E**3), 0 if transposed else 1)
    sub, cell = row // 64, row % 64
    a = (cell // 16) * 2 + sub // 4
    b = (cell // 4) % 4 * 2 + (sub // 2) % 2
    c = cell % 4 * 2 + sub % 2
    return jnp.where(column == (a * 8 + b) * 8 + c, 1.0, 0.0).astype(BF16)


def dot(a, b, dims):
    return lax.dot_general(a, b, (dims, ((), ())), preferred_element_type=F32)


def forward_kernel(
    width_x,
    width_y,
    occupancy,
    offsets,
    rank,
    features,
    hx,
    hy,
    hc,
    received,
    w_sub,
    w_down,
    pre_grad,
    moved,
    partial,
    returned,
    ext,
    ext_t,
    weights,
    preact,
    patches,
    hidden_grad,
    acc,
):
    bricks = width_x * width_y
    wide = width_y + 2
    order = voxel_order(False)
    cells = [(x, y) for x in range(-1, width_x + 1) for y in range(-1, width_y + 1)]
    refs = (features, hx, hy, hc)
    for first in range(0, len(cells), 2):
        pair = []
        for x, y in cells[first : first + 2]:
            ref, at = ext_source(width_x, width_y, refs, x, y)
            pair.append(ref[at])
        moved_pair = dot(order, jnp.concatenate(pair, 1), ((1,), (0,))).astype(BF16)
        for j in range(2):
            column = moved_pair[:, j * 128 : (j + 1) * 128]
            ext[first + j] = column
            ext_t[first + j] = column.T
    for p in range(bricks):
        returned[pl.ds(p * 64, 64)] = received[rank[p]]
    acc[...] = jnp.zeros_like(acc)

    def spread(g, _):
        rows = pl.ds(pl.multiple_of(g * 256, 256), 256)
        hidden_grad[rows] = dot(returned[rows], w_down[...], ((1,), (1,)))
        return 0

    lax.fori_loop(0, bricks // 4, spread, 0)

    def brick(p, _):
        x, y = p // width_y, p % width_y
        rows = pl.ds(pl.multiple_of(p * 64, 64), 64)
        present = occupancy[p].astype(F32)
        at = [(x + 1 + dx) * wide + y + 1 + dy for dx, dy in NEIGHBOURS]
        codes = [offsets[p * 9 + k] for k in range(9)]
        for k in range(9):
            chosen = w_sub[jnp.minimum(codes[k], 26)]
            weights[pl.ds(k * 128, 128)] = jnp.where(codes[k] < 27, chosen, jnp.zeros_like(chosen))
        window = jnp.concatenate([ext[i] for i in at], 1)
        preact[...] = dot(window, weights[...], ((1,), (0,)))
        for s in range(8):
            part = pl.ds(s * 64, 64)
            lanes = pl.ds(s * 128, 128)
            pre = preact[part]
            sig = jax.nn.sigmoid(pre)
            own = ext[at[4], part].astype(F32)
            patches[rows, lanes] = (present * (own + pre * sig)).astype(BF16)
            slope = sig * (1.0 + pre * (1.0 - sig))
            pre_grad[p, part] = (present * hidden_grad[rows, lanes] * slope).astype(BF16)
        window_t = jnp.concatenate([ext_t[i] for i in at], 0)
        outer = dot(window_t, pre_grad[p], ((1,), (0,)))
        for k in range(9):
            acc[codes[k]] += outer[k * 128 : (k + 1) * 128]
        return 0

    lax.fori_loop(0, bricks, brick, 0)
    shifted = dot(patches[...], w_down[...], ((1,), (0,))).astype(BF16)
    for p in range(bricks):
        moved[rank[p]] = shifted[p * 64 : (p + 1) * 64]
    for o in range(27):
        partial[pl.ds(o * 128, 128)] = acc[o]
    top = 27 * 128
    for s in range(8):
        grad = dot(patches[:, s * 128 : (s + 1) * 128], returned[...], ((0,), (0,)))
        for half in range(2):
            partial[pl.ds(top + half * 1024 + s * 128, 128)] = grad[:, half * 128 : half * 128 + 128]
    top += 2048
    if partial.shape[0] > top:
        partial[pl.ds(top, partial.shape[0] - top)] = jnp.zeros(
            (partial.shape[0] - top, 128), F32
        )


def backward_kernel(
    width_x,
    width_y,
    devices,
    occupancy,
    offsets,
    rank,
    pre_grad,
    hx,
    hy,
    hc,
    returned,
    received,
    total,
    w_sub,
    w_down,
    coarse,
    feature_grad,
    sub_grad,
    down_grad,
    ext,
    weights,
    hidden_grad,
):
    bricks = width_x * width_y
    wide = width_y + 2
    refs = (pre_grad, hx, hy, hc)
    cells = [(x, y) for x in range(-1, width_x + 1) for y in range(-1, width_y + 1)]
    for i, (x, y) in enumerate(cells):
        ref, at = ext_source(width_x, width_y, refs, x, y)
        ext[i] = ref[at]
    for p in range(bricks):
        coarse[p // width_y, p % width_y] = received[rank[p]]
    scale = 1.0 / devices
    for o in range(27):
        sub_grad[o] = total[pl.ds(o * 128, 128)].astype(F32) * scale
    for half in range(2):
        down_grad[:, pl.ds(half * 128, 128)] = (
            total[pl.ds(27 * 128 + half * 1024, 1024)].astype(F32) * scale
        )

    def spread(g, _):
        rows = pl.ds(pl.multiple_of(g * 256, 256), 256)
        hidden_grad[rows] = dot(returned[rows], w_down[...], ((1,), (1,)))
        return 0

    lax.fori_loop(0, bricks // 4, spread, 0)
    back = voxel_order(True)

    def column(p, _):
        x, y = p // width_y, p % width_y
        at = [(x + 1 + dx) * wide + y + 1 + dy for dx, dy in NEIGHBOURS]
        for k in range(9):
            code = offsets[p * 9 + k]
            chosen = w_sub[jnp.maximum(26 - code, 0)]
            weights[:, k * 128 : (k + 1) * 128] = jnp.where(
                code < 27, chosen, jnp.zeros_like(chosen)
            )
        window = jnp.concatenate([ext[i] for i in at], 1)
        conv = dot(window, weights[...], ((1,), (1,)))
        rows = pl.ds(pl.multiple_of(p * 64, 64), 64)
        spread_rows = jnp.concatenate(
            [hidden_grad[rows, s * 128 : (s + 1) * 128] for s in range(8)], 0
        )
        return (occupancy[p].astype(F32) * (spread_rows + conv)).astype(BF16)

    def pair(i, _):
        p = i * 2
        both = jnp.concatenate([column(p, 0), column(p + 1, 0)], 1)
        out = dot(back, both, ((1,), (0,))).astype(BF16)
        feature_grad[p // width_y, p % width_y] = out[:, :128]
        feature_grad[(p + 1) // width_y, (p + 1) % width_y] = out[:, 128:]
        return 0

    lax.fori_loop(0, bricks // 2, pair, 0)


def ranks(keys):
    rank = jnp.sum((keys[None, :] < keys[:, None]).astype(jnp.int32), 1)
    places = jnp.arange(keys.shape[0], dtype=jnp.int32)
    order = jnp.sum((rank[None, :] == places[:, None]).astype(jnp.int32) * places[None, :], 1)
    return rank, order


def local(nx, ny, features, occupancy, pair_offset, owner, w_sub, w_down, cotangent):
    width_x, width_y, voxels, channels = features.shape
    bricks = width_x * width_y
    cells, out_channels = cotangent.shape[2:]
    share = bricks // nx
    occupied = occupancy.reshape(bricks)
    offsets = pair_offset.reshape(bricks * 9)
    targets = owner.reshape(bricks)
    places = jnp.arange(bricks, dtype=jnp.int32)
    source = (2 * lax.axis_index("gx") - targets + nx) % nx
    send_rank, _ = ranks(targets * bricks + places)
    cell_rank, cell_order = ranks(source * bricks + places)

    any_spec = pl.BlockSpec(memory_space=pl.ANY)
    vmem = pl.BlockSpec(memory_space=pltpu.VMEM)
    smem = pl.BlockSpec(memory_space=pltpu.SMEM)
    shape = jax.ShapeDtypeStruct
    halo_shapes = [
        shape((2, width_y, voxels, channels), BF16),
        shape((2, width_x, voxels, channels), BF16),
        shape((4, voxels, channels), BF16),
    ]
    block = shape((nx, share, cells, out_channels), BF16)
    dma = pltpu.SemaphoreType.DMA

    hx, hy, hc, received = pl.pallas_call(
        functools.partial(open_kernel, nx, ny),
        out_shape=halo_shapes + [block],
        in_specs=[smem, any_spec, vmem],
        out_specs=[any_spec] * 4,
        scratch_shapes=[
            pltpu.VMEM(block.shape, BF16),
            dma((9,)),
            dma((9,)),
            dma((nx,)),
            dma((nx,)),
        ],
        compiler_params=pltpu.CompilerParams(
            collective_id=0, has_side_effects=True, vmem_limit_bytes=VMEM_LIMIT
        ),
        name="open_exchange",
    )(cell_order, features, cotangent.reshape(bricks, cells, out_channels))

    unit = 16 * nx * ny
    rows = -(-(27 * channels + 2048) // unit) * unit
    brick_shape = (bricks, voxels, channels)
    pre_grad, moved, partial, returned = pl.pallas_call(
        functools.partial(forward_kernel, width_x, width_y),
        out_shape=[
            shape(brick_shape, BF16),
            shape((bricks, cells, out_channels), BF16),
            shape((rows, 128), F32),
            shape((bricks * cells, out_channels), BF16),
        ],
        in_specs=[smem] * 3 + [vmem] * 7,
        out_specs=[vmem] * 4,
        scratch_shapes=[
            pltpu.VMEM(((width_x + 2) * (width_y + 2), voxels, channels), BF16),
            pltpu.VMEM(((width_x + 2) * (width_y + 2), channels, voxels), BF16),
            pltpu.VMEM((9 * channels, channels), BF16),
            pltpu.VMEM((voxels, channels), F32),
            pltpu.VMEM((bricks * cells, 8 * channels), BF16),
            pltpu.VMEM((bricks * cells, 8 * channels), F32),
            pltpu.VMEM((28, channels, channels), F32),
        ],
        compiler_params=pltpu.CompilerParams(vmem_limit_bytes=VMEM_LIMIT),
        name="forward",
    )(
        occupied,
        offsets,
        send_rank,
        features,
        hx,
        hy,
        hc,
        received.reshape(bricks, cells, out_channels),
        w_sub,
        w_down,
    )

    plan = groups(nx, ny)
    buffers = []
    length = rows
    count = 0
    for _, _, size in plan:
        length //= size
        buffers.append(pltpu.VMEM((size - 1, length, 128), BF16))
        count += size - 1
    gx_halo, gy_halo, gc_halo, arrived, total = pl.pallas_call(
        functools.partial(close_kernel, nx, ny, len(plan)),
        out_shape=halo_shapes + [block, shape((rows, 128), BF16)],
        in_specs=[any_spec] * 3,
        out_specs=[any_spec] * 4 + [vmem],
        scratch_shapes=buffers
        + buffers
        + [
            pltpu.VMEM((rows, 128), F32),
            pltpu.VMEM((rows, 128), BF16),
            dma((9,)),
            dma((9,)),
            dma((nx,)),
            dma((nx,)),
            dma((count,)),
            dma((count,)),
            dma((count,)),
            dma((count,)),
            dma(()),
        ],
        compiler_params=pltpu.CompilerParams(
            collective_id=1, has_side_effects=True, vmem_limit_bytes=VMEM_LIMIT
        ),
        name="close_exchange",
    )(pre_grad.reshape(features.shape), moved.reshape(block.shape), partial)

    return pl.pallas_call(
        functools.partial(backward_kernel, width_x, width_y, nx * ny),
        out_shape=[
            shape(cotangent.shape, BF16),
            shape(features.shape, BF16),
            shape(w_sub.shape, F32),
            shape(w_down.shape, F32),
        ],
        in_specs=[smem] * 3 + [vmem] * 9,
        out_specs=[vmem] * 4,
        scratch_shapes=[
            pltpu.VMEM(((width_x + 2) * (width_y + 2), voxels, channels), BF16),
            pltpu.VMEM((channels, 9 * channels), BF16),
            pltpu.VMEM((bricks * cells, 8 * channels), F32),
        ],
        compiler_params=pltpu.CompilerParams(vmem_limit_bytes=VMEM_LIMIT),
        name="backward",
    )(
        occupied,
        offsets,
        cell_rank,
        pre_grad.reshape(features.shape),
        gx_halo,
        gy_halo,
        gc_halo,
        returned,
        arrived.reshape(bricks, cells, out_channels),
        total,
        w_sub,
        w_down,
    )


def solution(mesh):
    in_specs = (
        P("gx", "gy", None, None),
        P("gx", "gy"),
        P("gx", "gy", None),
        P("gx", "gy"),
        P(),
        P(),
        P("gx", "gy", None, None),
    )
    out_specs = (P("gx", "gy", None, None), P("gx", "gy", None, None), P(), P())
    return jax.shard_map(
        functools.partial(local, mesh.shape["gx"], mesh.shape["gy"]),
        mesh=mesh,
        in_specs=in_specs,
        out_specs=out_specs,
        check_vma=False,
    )
```

```python
import functools

import jax
import jax.numpy as jnp
from jax import lax
from jax.experimental import pallas as pl
from jax.experimental.pallas import tpu as pltpu
from jax.sharding import PartitionSpec as P

MESH = pl.DeviceIdType.MESH
E = 8
NEIGHBOURS = [(-1, -1), (-1, 0), (-1, 1), (0, -1), (0, 0), (0, 1), (1, -1), (1, 0), (1, 1)]
HALO = [k for k in range(9) if k != 4]
SEND_ORDER = [1, 7, 3, 5, 0, 2, 6, 8]
ALONG_Y = [3, 5]
ALONG_X = [1, 7, 0, 2, 6, 8]
F32 = jnp.float32
BF16 = jnp.bfloat16
VMEM_LIMIT = 58 * 1024 * 1024


def position():
    return lax.axis_index("gx"), lax.axis_index("gy")


def exists(nx, ny, gx, gy, k):
    dx, dy = NEIGHBOURS[k]
    x, y = gx + dx, gy + dy
    return (x >= 0) & (x < nx) & (y >= 0) & (y < ny)


def edge(ref, width_x, width_y, k):
    dx, dy = NEIGHBOURS[k]
    sx = {-1: 0, 0: slice(None), 1: width_x - 1}[dx]
    sy = {-1: 0, 0: slice(None), 1: width_y - 1}[dy]
    return ref.at[sx, sy]


def slot(halo, k):
    hx, hy, hc = halo
    dx, dy = NEIGHBOURS[k]
    if dy == 0:
        return hx.at[(dx + 1) // 2]
    if dx == 0:
        return hy.at[(dy + 1) // 2]
    return hc.at[(dx + 1) // 2 * 2 + (dy + 1) // 2]


def halo_copy(nx, ny, gx, gy, source, halo, send, recv, k):
    dx, dy = NEIGHBOURS[k]
    return pltpu.make_async_remote_copy(
        src_ref=edge(source, source.shape[0], source.shape[1], k),
        dst_ref=slot(halo, 8 - k),
        send_sem=send.at[k],
        recv_sem=recv.at[8 - k],
        device_id=(gx + dx, gy + dy),
        device_id_type=MESH,
    )


def halo_arrival(nx, ny, gx, gy, source, halo, send, recv, k):
    dx, dy = NEIGHBOURS[k]
    return pltpu.make_async_remote_copy(
        src_ref=edge(source, source.shape[0], source.shape[1], 8 - k),
        dst_ref=slot(halo, k),
        send_sem=send.at[8 - k],
        recv_sem=recv.at[k],
        device_id=(gx + dx, gy + dy),
        device_id_type=MESH,
    )


def halo_fill(source, halo, recv, k):
    return pltpu.make_async_copy(
        edge(source, source.shape[0], source.shape[1], k), slot(halo, k), recv.at[k]
    )


def start_halo(nx, ny, gx, gy, source, halo, send, recv):
    for k in SEND_ORDER:
        there = exists(nx, ny, gx, gy, k)

        @pl.when(there)
        def _(k=k):
            halo_copy(nx, ny, gx, gy, source, halo, send, recv, k).start()

        @pl.when(jnp.logical_not(there))
        def _(k=k):
            halo_fill(source, halo, recv, k).start()


def finish_halo(nx, ny, gx, gy, source, halo, send, recv, chosen):
    for k in chosen:
        there = exists(nx, ny, gx, gy, k)

        @pl.when(there)
        def _(k=k):
            halo_copy(nx, ny, gx, gy, source, halo, send, recv, k).wait_send()
            halo_arrival(nx, ny, gx, gy, source, halo, send, recv, k).wait_recv()

        @pl.when(jnp.logical_not(there))
        def _(k=k):
            halo_fill(source, halo, recv, k).wait()


def exchange_copy(nx, gx, gy, outgoing, incoming, send, recv, shift):
    peer = lax.rem(gx + shift, nx)
    return pltpu.make_async_remote_copy(
        src_ref=outgoing.at[peer],
        dst_ref=incoming.at[gx],
        send_sem=send.at[shift],
        recv_sem=recv.at[shift],
        device_id=(peer, gy),
        device_id_type=MESH,
    )


def exchange_arrival(nx, gx, gy, outgoing, incoming, send, recv, shift):
    peer = lax.rem(gx + nx - shift, nx)
    return pltpu.make_async_remote_copy(
        src_ref=outgoing.at[peer],
        dst_ref=incoming.at[peer],
        send_sem=send.at[shift],
        recv_sem=recv.at[shift],
        device_id=(peer, gy),
        device_id_type=MESH,
    )


def start_exchange(nx, gx, gy, outgoing, incoming, send, recv):
    pltpu.make_async_copy(outgoing.at[gx], incoming.at[gx], recv.at[0]).start()
    for shift in range(1, nx):
        exchange_copy(nx, gx, gy, outgoing, incoming, send, recv, shift).start()


def finish_exchange(nx, gx, gy, outgoing, incoming, send, recv):
    pltpu.make_async_copy(outgoing.at[gx], incoming.at[gx], recv.at[0]).wait()
    for shift in range(1, nx):
        exchange_copy(nx, gx, gy, outgoing, incoming, send, recv, shift).wait_send()
        exchange_arrival(nx, gx, gy, outgoing, incoming, send, recv, shift).wait_recv()


def greet(nx, ny, gx, gy, partners):
    barrier = pltpu.get_barrier_semaphore()
    for k in HALO:
        dx, dy = NEIGHBOURS[k]

        @pl.when(exists(nx, ny, gx, gy, k))
        def _(dx=dx, dy=dy):
            pl.semaphore_signal(
                barrier, inc=1, device_id=(gx + dx, gy + dy), device_id_type=MESH
            )

    for shift in range(1, nx):
        pl.semaphore_signal(
            barrier, inc=1, device_id=(lax.rem(gx + shift, nx), gy), device_id_type=MESH
        )
    for partner in partners:
        pl.semaphore_signal(barrier, inc=1, device_id=partner, device_id_type=MESH)
    count = nx - 1 + len(partners)
    for k in HALO:
        count = count + jnp.where(exists(nx, ny, gx, gy, k), 1, 0)
    pl.semaphore_wait(barrier, count)


def groups(nx, ny):
    deep = 4 if nx % 4 == 0 else 1
    return [
        (axis, stride, size)
        for axis, stride, size in (
            (1, 1, 2),
            (1, 2, ny // 2),
            (0, 1, nx // deep),
            (0, nx // deep, deep),
        )
        if size > 1
    ]


def member(gx, gy, group, shift):
    axis, stride, size = group
    here = (gx, gy)[axis]
    own = lax.rem(lax.div(here, stride), size)
    other = lax.rem(own + shift, size)
    there = here + (other - own) * stride
    return own, other, ((there, gy) if axis == 0 else (gx, there))


def reduce_all(nx, ny, gx, gy, partial, total, sends, recvs, ss, rs, gs, gr, fill):
    rows = partial.shape[0]
    plan = groups(nx, ny)
    base, length = 0, rows
    bases = []
    sem = 0
    for stage, group in enumerate(plan):
        size = group[2]
        chunk = length // size
        copies = []
        own = None
        for shift in range(1, size):
            own, other, device = member(gx, gy, group, shift)
            start = pl.multiple_of(base + other * chunk, 16)
            sends[stage][shift - 1] = partial[pl.ds(start, chunk)].astype(BF16)
            copy = pltpu.make_async_remote_copy(
                src_ref=sends[stage].at[shift - 1],
                dst_ref=recvs[stage].at[shift - 1],
                send_sem=ss.at[sem],
                recv_sem=rs.at[sem],
                device_id=device,
                device_id_type=MESH,
            )
            copy.start()
            copies.append(copy)
            sem += 1
        bases.append(base)
        base = pl.multiple_of(base + own * chunk, 16)
        length = chunk
        fill("scatter", stage)
        for copy in copies:
            copy.wait()
        value = partial[pl.ds(base, chunk)]
        for shift in range(1, size):
            value = value + recvs[stage][shift - 1].astype(F32)
        partial[pl.ds(base, chunk)] = value
    total[pl.ds(base, length)] = (partial[pl.ds(base, length)]).astype(BF16)
    sem = 0
    for stage in reversed(range(len(plan))):
        group = plan[stage]
        size = group[2]
        copies = []
        for shift in range(1, size):
            own, other, device = member(gx, gy, group, shift)
            back = lax.rem(own + size - shift, size)
            copies.append(
                (
                    pltpu.make_async_remote_copy(
                        src_ref=total.at[pl.ds(base, length)],
                        dst_ref=total.at[pl.ds(base, length)],
                        send_sem=gs.at[sem],
                        recv_sem=gr.at[sem],
                        device_id=device,
                        device_id_type=MESH,
                    ),
                    pl.multiple_of(bases[stage] + back * length, 16),
                    sem,
                    device,
                )
            )
            copies[-1][0].start()
            sem += 1
        fill("gather", stage)
        for copy, start, index, device in copies:
            copy.wait_send()
            pltpu.make_async_remote_copy(
                src_ref=total.at[pl.ds(base, length)],
                dst_ref=total.at[pl.ds(start, length)],
                send_sem=gs.at[index],
                recv_sem=gr.at[index],
                device_id=device,
                device_id_type=MESH,
            ).wait_recv()
        base = bases[stage]
        length = length * size


def ext_source(width_x, width_y, refs, x, y):
    own, hx, hy, hc = refs
    sx = 0 if x < 0 else (2 if x >= width_x else 1)
    sy = 0 if y < 0 else (2 if y >= width_y else 1)
    if sx == 1 and sy == 1:
        return own, (x, y)
    if sy == 1:
        return hx, (sx // 2, y)
    if sx == 1:
        return hy, (sy // 2, x)
    return hc, (sx // 2 * 2 + sy // 2,)


def voxel_order(transposed):
    row = lax.broadcasted_iota(jnp.int32, (E**3, E**3), 1 if transposed else 0)
    column = lax.broadcasted_iota(jnp.int32, (E**3, E**3), 0 if transposed else 1)
    sub, cell = row // 64, row % 64
    a = (cell // 16) * 2 + sub // 4
    b = (cell // 4) % 4 * 2 + (sub // 2) % 2
    c = cell % 4 * 2 + sub % 2
    return jnp.where(column == (a * 8 + b) * 8 + c, 1.0, 0.0).astype(BF16)


def dot(a, b, dims):
    return lax.dot_general(a, b, (dims, ((), ())), preferred_element_type=F32)


def whole_kernel(
    nx,
    ny,
    stages,
    occupancy,
    offsets,
    send_rank,
    send_order,
    cell_rank,
    cell_order,
    features,
    cotangent,
    w_sub,
    w_down,
    coarse,
    feature_grad,
    sub_grad,
    down_grad,
    *scratch,
):
    sends, recvs = scratch[:stages], scratch[stages : 2 * stages]
    (
        hx, hy, hc, gx_halo, gy_halo, gc_halo,
        outgoing, incoming, leaving, arrived,
        pre_grad, ext, ext_t, weights, back_weights, preact, patches, hidden_grad,
        returned, shifted, partial, total,
        hs, hr, es, er, ps, pr, ms, mr, ss, rs, gs, gr,
    ) = scratch[2 * stages :]
    width_x, width_y = features.shape[:2]
    bricks = width_x * width_y
    wide = width_y + 2
    share = outgoing.shape[1]
    gx, gy = position()
    halo = (hx, hy, hc)
    grad_halo = (gx_halo, gy_halo, gc_halo)
    plan = groups(nx, ny)
    partners = [
        member(gx, gy, group, shift)[2] for group in plan for shift in range(1, group[2])
    ]
    greet(nx, ny, gx, gy, partners)
    start_halo(nx, ny, gx, gy, features, halo, hs, hr)
    for i in range(bricks):
        outgoing[i // share, i % share] = cotangent[cell_order[i]]
    start_exchange(nx, gx, gy, outgoing, incoming, es, er)

    order = voxel_order(False)
    cells = [(x, y) for x in range(-1, width_x + 1) for y in range(-1, width_y + 1)]
    own = [(x, y) for x, y in cells if 0 <= x < width_x and 0 <= y < width_y]
    beside = [(x, y) for x, y in cells if 0 <= x < width_x and not 0 <= y < width_y]
    outer_rows = [(x, y) for x, y in cells if not 0 <= x < width_x]

    def place(refs, chosen):
        for first in range(0, len(chosen), 2):
            pair = []
            for x, y in chosen[first : first + 2]:
                ref, at = ext_source(width_x, width_y, refs, x, y)
                pair.append(ref[at])
            both = dot(order, jnp.concatenate(pair, 1), ((1,), (0,))).astype(BF16)
            for j, (x, y) in enumerate(chosen[first : first + 2]):
                column = both[:, j * 128 : (j + 1) * 128]
                i = (x + 1) * wide + y + 1
                ext[i] = column
                ext_t[i] = column.T

    refs = (features, hx, hy, hc)
    place(refs, own)
    partial[...] = jnp.zeros_like(partial)
    finish_exchange(nx, gx, gy, outgoing, incoming, es, er)
    for p in range(bricks):
        rank = send_rank[p]
        returned[pl.ds(p * 64, 64)] = incoming[rank // share, rank % share]

    def spread(g, _):
        rows = pl.ds(pl.multiple_of(g * 256, 256), 256)
        hidden_grad[rows] = dot(returned[rows], w_down[...], ((1,), (1,)))
        return 0

    lax.fori_loop(0, bricks // 4, spread, 0)
    finish_halo(nx, ny, gx, gy, features, halo, hs, hr, ALONG_Y)
    place(refs, beside)

    def windows(p):
        x, y = p // width_y, p % width_y
        return x, y, [(x + 1 + dx) * wide + y + 1 + dy for dx, dy in NEIGHBOURS]

    def forward(p):
        x, y, at = windows(p)
        rows = pl.ds(pl.multiple_of(p * 64, 64), 64)
        present = occupancy[p].astype(F32)
        for k in range(9):
            code = offsets[p * 9 + k]
            chosen = w_sub[jnp.minimum(code, 26)]
            weights[pl.ds(k * 128, 128)] = jnp.where(code < 27, chosen, jnp.zeros_like(chosen))
        window = jnp.concatenate([ext[i] for i in at], 1)
        preact[...] = dot(window, weights[...], ((1,), (0,)))
        for s in range(8):
            part = pl.ds(s * 64, 64)
            lanes = pl.ds(s * 128, 128)
            pre = preact[part]
            sig = jax.nn.sigmoid(pre)
            centre = ext[at[4], part].astype(F32)
            patches[rows, lanes] = (present * (centre + pre * sig)).astype(BF16)
            slope = sig * (1.0 + pre * (1.0 - sig))
            pre_grad[x, y, part] = (present * hidden_grad[rows, lanes] * slope).astype(BF16)

    def kernel_grad(p):
        x, y, at = windows(p)
        window_t = jnp.concatenate([ext_t[i] for i in at], 0)
        outer = dot(window_t, pre_grad[x, y], ((1,), (0,)))
        for k in range(9):
            code = offsets[p * 9 + k]
            term = outer[k * 128 : (k + 1) * 128]
            for o in range(3 * k, 3 * k + 3):
                here = pl.ds(o * 128, 128)
                partial[here] = partial[here] + jnp.where(code == o, term, jnp.zeros_like(term))

    def inner_step(i, _):
        forward(i + width_y)
        kernel_grad(i + width_y)
        return 0

    middle = bricks - 2 * width_y
    lax.fori_loop(0, middle, inner_step, 0)
    finish_halo(nx, ny, gx, gy, features, halo, hs, hr, ALONG_X)
    place(refs, outer_rows)

    def rim(i):
        return i + (i // width_y) * middle

    def rim_forward(i, _):
        forward(rim(i))
        return 0

    lax.fori_loop(0, 2 * width_y, rim_forward, 0)
    start_halo(nx, ny, gx, gy, pre_grad, grad_halo, ps, pr)

    down = dot(patches[...], w_down[...], ((1,), (0,))).astype(BF16)
    for p in range(bricks):
        shifted[p] = down[p * 64 : (p + 1) * 64]
    for i in range(bricks):
        leaving[i // share, i % share] = shifted[send_order[i]]
    start_exchange(nx, gx, gy, leaving, arrived, ms, mr)

    def rim_grad(i, _):
        kernel_grad(rim(i))
        return 0

    lax.fori_loop(0, 2 * width_y, rim_grad, 0)
    top = 27 * 128
    for s in range(8):
        grad = dot(patches[:, s * 128 : (s + 1) * 128], returned[...], ((0,), (0,)))
        for half in range(2):
            partial[pl.ds(top + half * 1024 + s * 128, 128)] = grad[:, half * 128 : half * 128 + 128]

    back = voxel_order(True)
    grad_refs = (pre_grad, gx_halo, gy_halo, gc_halo)

    def lay(chosen):
        for x, y in chosen:
            ref, at = ext_source(width_x, width_y, grad_refs, x, y)
            ext[(x + 1) * wide + y + 1] = ref[at]

    def column(p):
        x, y, at = windows(p)
        for k in range(9):
            code = offsets[p * 9 + k]
            chosen = w_sub[jnp.maximum(26 - code, 0)]
            back_weights[:, k * 128 : (k + 1) * 128] = jnp.where(
                code < 27, chosen, jnp.zeros_like(chosen)
            )
        window = jnp.concatenate([ext[i] for i in at], 1)
        conv = dot(window, back_weights[...], ((1,), (1,)))
        rows = pl.ds(pl.multiple_of(p * 64, 64), 64)
        spread_rows = jnp.concatenate(
            [hidden_grad[rows, s * 128 : (s + 1) * 128] for s in range(8)], 0
        )
        return (occupancy[p].astype(F32) * (spread_rows + conv)).astype(BF16)

    def pair(i, _):
        p = i * 2
        both = jnp.concatenate([column(p), column(p + 1)], 1)
        out = dot(back, both, ((1,), (0,))).astype(BF16)
        feature_grad[p // width_y, p % width_y] = out[:, :128]
        feature_grad[(p + 1) // width_y, (p + 1) % width_y] = out[:, 128:]
        return 0

    per_row = width_y // 2
    last = bricks // 2
    half = last // 2

    def fill(phase, stage):
        if phase == "scatter" and stage == 0:
            lay(own)
            finish_halo(nx, ny, gx, gy, pre_grad, grad_halo, ps, pr, ALONG_Y)
            lay(beside)
        if phase == "scatter" and stage == 1:
            lax.fori_loop(per_row, last - per_row, pair, 0)
        if phase == "gather" and stage == 1:
            finish_halo(nx, ny, gx, gy, pre_grad, grad_halo, ps, pr, ALONG_X)
            lay(outer_rows)

            def rim_pair(i, _):
                return pair(i + (i // per_row) * (last - 2 * per_row), 0)

            lax.fori_loop(0, 2 * per_row, rim_pair, 0)
        if phase == "gather" and stage == 0:
            finish_exchange(nx, gx, gy, leaving, arrived, ms, mr)
            for p in range(bricks):
                rank = cell_rank[p]
                coarse[p // width_y, p % width_y] = arrived[rank // share, rank % share]

    reduce_all(nx, ny, gx, gy, partial, total, sends, recvs, ss, rs, gs, gr, fill)
    scale = 1.0 / (nx * ny)
    for o in range(27):
        sub_grad[o] = total[pl.ds(o * 128, 128)].astype(F32) * scale
    for side in range(2):
        down_grad[:, pl.ds(side * 128, 128)] = (
            total[pl.ds(top + side * 1024, 1024)].astype(F32) * scale
        )


def ranks(keys):
    rank = jnp.sum((keys[None, :] < keys[:, None]).astype(jnp.int32), 1)
    places = jnp.arange(keys.shape[0], dtype=jnp.int32)
    order = jnp.sum((rank[None, :] == places[:, None]).astype(jnp.int32) * places[None, :], 1)
    return rank, order


def local(nx, ny, features, occupancy, pair_offset, owner, w_sub, w_down, cotangent):
    width_x, width_y, voxels, channels = features.shape
    bricks = width_x * width_y
    cells, out_channels = cotangent.shape[2:]
    share = bricks // nx
    occupied = occupancy.reshape(bricks)
    offsets = pair_offset.reshape(bricks * 9)
    targets = owner.reshape(bricks)
    places = jnp.arange(bricks, dtype=jnp.int32)
    source = (2 * lax.axis_index("gx") - targets + nx) % nx
    send_rank, send_order = ranks(targets * bricks + places)
    cell_rank, cell_order = ranks(source * bricks + places)

    vmem = pl.BlockSpec(memory_space=pltpu.VMEM)
    smem = pl.BlockSpec(memory_space=pltpu.SMEM)
    shape = jax.ShapeDtypeStruct
    dma = pltpu.SemaphoreType.DMA
    halo_buffers = [
        pltpu.VMEM((2, width_y, voxels, channels), BF16),
        pltpu.VMEM((2, width_x, voxels, channels), BF16),
        pltpu.VMEM((4, voxels, channels), BF16),
    ]
    block = pltpu.VMEM((nx, share, cells, out_channels), BF16)
    unit = 16 * nx * ny
    rows = -(-(27 * channels + 2048) // unit) * unit
    plan = groups(nx, ny)
    buffers = []
    length = rows
    count = 0
    for _, _, size in plan:
        length //= size
        buffers.append(pltpu.VMEM((size - 1, length, 128), BF16))
        count += size - 1
    around = (width_x + 2) * (width_y + 2)
    return pl.pallas_call(
        functools.partial(whole_kernel, nx, ny, len(plan)),
        out_shape=[
            shape(cotangent.shape, BF16),
            shape(features.shape, BF16),
            shape(w_sub.shape, F32),
            shape(w_down.shape, F32),
        ],
        in_specs=[smem] * 6 + [vmem] * 4,
        out_specs=[vmem] * 4,
        scratch_shapes=buffers
        + buffers
        + halo_buffers
        + halo_buffers
        + [block] * 4
        + [
            pltpu.VMEM(features.shape, BF16),
            pltpu.VMEM((around, voxels, channels), BF16),
            pltpu.VMEM((around, channels, voxels), BF16),
            pltpu.VMEM((9 * channels, channels), BF16),
            pltpu.VMEM((channels, 9 * channels), BF16),
            pltpu.VMEM((voxels, channels), F32),
            pltpu.VMEM((bricks * cells, 8 * channels), BF16),
            pltpu.VMEM((bricks * cells, 8 * channels), F32),
            pltpu.VMEM((bricks * cells, out_channels), BF16),
            pltpu.VMEM((bricks, cells, out_channels), BF16),
            pltpu.VMEM((rows, 128), F32),
            pltpu.VMEM((rows, 128), BF16),
        ]
        + [dma((9,)), dma((9,)), dma((nx,)), dma((nx,))] * 2
        + [dma((count,))] * 4,
        compiler_params=pltpu.CompilerParams(
            collective_id=0, has_side_effects=True, vmem_limit_bytes=VMEM_LIMIT
        ),
        name="section",
    )(
        occupied,
        offsets,
        send_rank,
        send_order,
        cell_rank,
        cell_order,
        features,
        cotangent.reshape(bricks, cells, out_channels),
        w_sub,
        w_down,
    )


def solution(mesh):
    in_specs = (
        P("gx", "gy", None, None),
        P("gx", "gy"),
        P("gx", "gy", None),
        P("gx", "gy"),
        P(),
        P(),
        P("gx", "gy", None, None),
    )
    out_specs = (P("gx", "gy", None, None), P("gx", "gy", None, None), P(), P())
    return jax.shard_map(
        functools.partial(local, mesh.shape["gx"], mesh.shape["gy"]),
        mesh=mesh,
        in_specs=in_specs,
        out_specs=out_specs,
        check_vma=False,
    )
```

```python
import functools

import jax
import jax.numpy as jnp
from jax import lax
from jax.experimental import pallas as pl
from jax.experimental.pallas import tpu as pltpu
from jax.sharding import PartitionSpec as P

MESH = pl.DeviceIdType.MESH
E = 8
NEIGHBOURS = [(-1, -1), (-1, 0), (-1, 1), (0, -1), (0, 0), (0, 1), (1, -1), (1, 0), (1, 1)]
ALONG_X = [1, 7]
ALONG_Y = [3, 5]
HALO = ALONG_X + ALONG_Y
F32 = jnp.float32
BF16 = jnp.bfloat16
VMEM_LIMIT = 58 * 1024 * 1024


def position():
    return lax.axis_index("gx"), lax.axis_index("gy")


def exists(nx, ny, gx, gy, k):
    dx, dy = NEIGHBOURS[k]
    x, y = gx + dx, gy + dy
    return (x >= 0) & (x < nx) & (y >= 0) & (y < ny)


def edge(ref, width_x, width_y, k):
    dx, dy = NEIGHBOURS[k]
    sx = {-1: 0, 0: slice(None), 1: width_x - 1}[dx]
    sy = {-1: 0, 0: slice(None), 1: width_y - 1}[dy]
    return ref.at[sx, sy]


def slot(halo, k):
    hx, hy, hc = halo
    dx, dy = NEIGHBOURS[k]
    if dy == 0:
        return hx.at[(dx + 1) // 2]
    if dx == 0:
        return hy.at[(dy + 1) // 2]
    return hc.at[(dx + 1) // 2 * 2 + (dy + 1) // 2]


def halo_copy(nx, ny, gx, gy, source, halo, send, recv, k):
    dx, dy = NEIGHBOURS[k]
    return pltpu.make_async_remote_copy(
        src_ref=edge(source, source.shape[0], source.shape[1], k),
        dst_ref=slot(halo, 8 - k),
        send_sem=send.at[k],
        recv_sem=recv.at[8 - k],
        device_id=(gx + dx, gy + dy),
        device_id_type=MESH,
    )


def halo_arrival(nx, ny, gx, gy, source, halo, send, recv, k):
    dx, dy = NEIGHBOURS[k]
    return pltpu.make_async_remote_copy(
        src_ref=edge(source, source.shape[0], source.shape[1], 8 - k),
        dst_ref=slot(halo, k),
        send_sem=send.at[8 - k],
        recv_sem=recv.at[k],
        device_id=(gx + dx, gy + dy),
        device_id_type=MESH,
    )


def halo_fill(source, halo, recv, k):
    return pltpu.make_async_copy(
        edge(source, source.shape[0], source.shape[1], k), slot(halo, k), recv.at[k]
    )


def start_halo(nx, ny, gx, gy, source, halo, send, recv, chosen):
    for k in chosen:
        there = exists(nx, ny, gx, gy, k)

        @pl.when(there)
        def _(k=k):
            halo_copy(nx, ny, gx, gy, source, halo, send, recv, k).start()

        @pl.when(jnp.logical_not(there))
        def _(k=k):
            halo_fill(source, halo, recv, k).start()


def finish_halo(nx, ny, gx, gy, source, halo, send, recv, chosen):
    for k in chosen:
        there = exists(nx, ny, gx, gy, k)

        @pl.when(there)
        def _(k=k):
            halo_copy(nx, ny, gx, gy, source, halo, send, recv, k).wait_send()
            halo_arrival(nx, ny, gx, gy, source, halo, send, recv, k).wait_recv()

        @pl.when(jnp.logical_not(there))
        def _(k=k):
            halo_fill(source, halo, recv, k).wait()


def corner_copy(gx, gy, halo, send, recv, side, dy):
    hx, _, hc = halo
    dx = 2 * side - 1
    column = 0 if dy < 0 else hx.shape[1] - 1
    here, there = 3 * (dx + 1) + dy + 1, 3 * (dx + 1) - dy + 1
    return pltpu.make_async_remote_copy(
        src_ref=hx.at[side, column],
        dst_ref=hc.at[2 * side + (1 - dy) // 2],
        send_sem=send.at[here],
        recv_sem=recv.at[there],
        device_id=(gx, gy + dy),
        device_id_type=MESH,
    )


def corner_arrival(gx, gy, halo, send, recv, side, dy):
    hx, _, hc = halo
    k = 3 * 2 * side + dy + 1
    return pltpu.make_async_remote_copy(
        src_ref=hx.at[side, 0],
        dst_ref=hc.at[2 * side + (1 + dy) // 2],
        send_sem=send.at[k],
        recv_sem=recv.at[k],
        device_id=(gx, gy + dy),
        device_id_type=MESH,
    )


def corner_fill(halo, recv, side, dy):
    hx, _, hc = halo
    return pltpu.make_async_copy(
        hx.at[side, 0], hc.at[2 * side + (1 + dy) // 2], recv.at[3 * 2 * side + dy + 1]
    )


def start_corners(ny, gx, gy, halo, send, recv):
    for side in range(2):
        for dy in (-1, 1):
            there = (gy + dy >= 0) & (gy + dy < ny)

            @pl.when(there)
            def _(side=side, dy=dy):
                corner_copy(gx, gy, halo, send, recv, side, dy).start()

            @pl.when(jnp.logical_not(there))
            def _(side=side, dy=dy):
                corner_fill(halo, recv, side, dy).start()


def finish_corners(ny, gx, gy, halo, send, recv):
    for side in range(2):
        for dy in (-1, 1):
            there = (gy + dy >= 0) & (gy + dy < ny)

            @pl.when(there)
            def _(side=side, dy=dy):
                corner_copy(gx, gy, halo, send, recv, side, dy).wait_send()
                corner_arrival(gx, gy, halo, send, recv, side, dy).wait_recv()

            @pl.when(jnp.logical_not(there))
            def _(side=side, dy=dy):
                corner_fill(halo, recv, side, dy).wait()


def exchange_copy(nx, gx, gy, outgoing, incoming, send, recv, shift):
    peer = lax.rem(gx + shift, nx)
    return pltpu.make_async_remote_copy(
        src_ref=outgoing.at[peer],
        dst_ref=incoming.at[gx],
        send_sem=send.at[shift],
        recv_sem=recv.at[shift],
        device_id=(peer, gy),
        device_id_type=MESH,
    )


def exchange_arrival(nx, gx, gy, outgoing, incoming, send, recv, shift):
    peer = lax.rem(gx + nx - shift, nx)
    return pltpu.make_async_remote_copy(
        src_ref=outgoing.at[peer],
        dst_ref=incoming.at[peer],
        send_sem=send.at[shift],
        recv_sem=recv.at[shift],
        device_id=(peer, gy),
        device_id_type=MESH,
    )


def start_exchange(nx, gx, gy, outgoing, incoming, send, recv):
    pltpu.make_async_copy(outgoing.at[gx], incoming.at[gx], recv.at[0]).start()
    for shift in range(1, nx):
        exchange_copy(nx, gx, gy, outgoing, incoming, send, recv, shift).start()


def finish_exchange(nx, gx, gy, outgoing, incoming, send, recv):
    pltpu.make_async_copy(outgoing.at[gx], incoming.at[gx], recv.at[0]).wait()
    for shift in range(1, nx):
        exchange_copy(nx, gx, gy, outgoing, incoming, send, recv, shift).wait_send()
        exchange_arrival(nx, gx, gy, outgoing, incoming, send, recv, shift).wait_recv()


def greet(nx, ny, gx, gy, partners):
    barrier = pltpu.get_barrier_semaphore()
    for k in HALO:
        dx, dy = NEIGHBOURS[k]

        @pl.when(exists(nx, ny, gx, gy, k))
        def _(dx=dx, dy=dy):
            pl.semaphore_signal(
                barrier, inc=1, device_id=(gx + dx, gy + dy), device_id_type=MESH
            )

    for shift in range(1, nx):
        pl.semaphore_signal(
            barrier, inc=1, device_id=(lax.rem(gx + shift, nx), gy), device_id_type=MESH
        )
    for partner in partners:
        pl.semaphore_signal(barrier, inc=1, device_id=partner, device_id_type=MESH)
    count = nx - 1 + len(partners)
    for k in HALO:
        count = count + jnp.where(exists(nx, ny, gx, gy, k), 1, 0)
    pl.semaphore_wait(barrier, count)


def groups(nx, ny):
    deep = 4 if nx % 4 == 0 else 1
    return [
        (axis, stride, size)
        for axis, stride, size in (
            (1, 1, 2),
            (1, 2, ny // 2),
            (0, 1, nx // deep),
            (0, nx // deep, deep),
        )
        if size > 1
    ]


def member(gx, gy, group, shift):
    axis, stride, size = group
    here = (gx, gy)[axis]
    own = lax.rem(lax.div(here, stride), size)
    other = lax.rem(own + shift, size)
    there = here + (other - own) * stride
    return own, other, ((there, gy) if axis == 0 else (gx, there))


def pieces(nx, ny, rows):
    plan = groups(nx, ny)
    unit = 16 * nx * ny
    first = rows // unit // 2 * unit
    turned = plan[:1] + plan[1:-1][::-1] + plan[-1:]
    return [(0, first, plan), (first, rows - first, turned)]


def reduce_all(nx, ny, gx, gy, partial, total, sends, recvs, ss, rs, gs, gr, fill):
    work = pieces(nx, ny, partial.shape[0])
    stages = len(work[0][2])
    base = [start for start, _, _ in work]
    length = [count for _, count, _ in work]
    bases = [[] for _ in work]
    sem = 0
    for stage in range(stages):
        copies = []
        for w, (_, _, plan) in enumerate(work):
            group = plan[stage]
            size = group[2]
            chunk = length[w] // size
            buffer = w * stages + stage
            for shift in range(1, size):
                own, other, device = member(gx, gy, group, shift)
                start = pl.multiple_of(base[w] + other * chunk, 16)
                sends[buffer][shift - 1] = partial[pl.ds(start, chunk)].astype(BF16)
                copy = pltpu.make_async_remote_copy(
                    src_ref=sends[buffer].at[shift - 1],
                    dst_ref=recvs[buffer].at[shift - 1],
                    send_sem=ss.at[sem],
                    recv_sem=rs.at[sem],
                    device_id=device,
                    device_id_type=MESH,
                )
                copy.start()
                copies.append(copy)
                sem += 1
            bases[w].append(base[w])
            base[w] = pl.multiple_of(base[w] + own * chunk, 16)
            length[w] = chunk
        fill("scatter", stage)
        for copy in copies:
            copy.wait()
        for w, (_, _, plan) in enumerate(work):
            buffer = w * stages + stage
            here = pl.ds(base[w], length[w])
            value = partial[here]
            for shift in range(1, plan[stage][2]):
                value = value + recvs[buffer][shift - 1].astype(F32)
            partial[here] = value
    for w in range(len(work)):
        here = pl.ds(base[w], length[w])
        total[here] = partial[here].astype(BF16)
    sem = 0
    for stage in reversed(range(stages)):
        copies = []
        for w, (_, _, plan) in enumerate(work):
            group = plan[stage]
            size = group[2]
            here = pl.ds(base[w], length[w])
            for shift in range(1, size):
                own, other, device = member(gx, gy, group, shift)
                back = lax.rem(own + size - shift, size)
                landing = pl.multiple_of(bases[w][stage] + back * length[w], 16)
                copy = pltpu.make_async_remote_copy(
                    src_ref=total.at[here],
                    dst_ref=total.at[here],
                    send_sem=gs.at[sem],
                    recv_sem=gr.at[sem],
                    device_id=device,
                    device_id_type=MESH,
                )
                copy.start()
                arrival = pltpu.make_async_remote_copy(
                    src_ref=total.at[here],
                    dst_ref=total.at[pl.ds(landing, length[w])],
                    send_sem=gs.at[sem],
                    recv_sem=gr.at[sem],
                    device_id=device,
                    device_id_type=MESH,
                )
                copies.append((copy, arrival))
                sem += 1
        fill("gather", stage)
        for copy, arrival in copies:
            copy.wait_send()
            arrival.wait_recv()
        for w, (_, _, plan) in enumerate(work):
            base[w] = bases[w][stage]
            length[w] = length[w] * plan[stage][2]


def ext_source(width_x, width_y, refs, x, y):
    own, hx, hy, hc = refs
    sx = 0 if x < 0 else (2 if x >= width_x else 1)
    sy = 0 if y < 0 else (2 if y >= width_y else 1)
    if sx == 1 and sy == 1:
        return own, (x, y)
    if sy == 1:
        return hx, (sx // 2, y)
    if sx == 1:
        return hy, (sy // 2, x)
    return hc, (sx // 2 * 2 + sy // 2,)


def voxel_order(transposed):
    row = lax.broadcasted_iota(jnp.int32, (E**3, E**3), 1 if transposed else 0)
    column = lax.broadcasted_iota(jnp.int32, (E**3, E**3), 0 if transposed else 1)
    sub, cell = row // 64, row % 64
    a = (cell // 16) * 2 + sub // 4
    b = (cell // 4) % 4 * 2 + (sub // 2) % 2
    c = cell % 4 * 2 + sub % 2
    return jnp.where(column == (a * 8 + b) * 8 + c, 1.0, 0.0).astype(BF16)


def dot(a, b, dims):
    return lax.dot_general(a, b, (dims, ((), ())), preferred_element_type=F32)


def whole_kernel(
    nx,
    ny,
    stages,
    occupancy,
    offsets,
    send_rank,
    send_order,
    cell_rank,
    cell_order,
    features,
    cotangent,
    w_sub,
    w_down,
    coarse,
    feature_grad,
    total,
    *scratch,
):
    buffers = 2 * stages
    sends, recvs = scratch[:buffers], scratch[buffers : 2 * buffers]
    (
        hx, hy, hc, gx_halo, gy_halo, gc_halo,
        outgoing, incoming, leaving, arrived,
        pre_grad, ext, ext_t, weights, back_weights, preact, patches, hidden_grad,
        returned, shifted, partial,
        hs, hr, es, er, ps, pr, ms, mr, ss, rs, gs, gr,
    ) = scratch[2 * buffers :]
    width_x, width_y = features.shape[:2]
    bricks = width_x * width_y
    wide = width_y + 2
    share = outgoing.shape[1]
    gx, gy = position()
    halo = (hx, hy, hc)
    grad_halo = (gx_halo, gy_halo, gc_halo)
    plan = groups(nx, ny)
    partners = [
        member(gx, gy, group, shift)[2] for group in plan for shift in range(1, group[2])
    ]
    greet(nx, ny, gx, gy, partners)
    start_halo(nx, ny, gx, gy, features, halo, hs, hr, HALO)
    for i in range(bricks):
        outgoing[i // share, i % share] = cotangent[cell_order[i]]
    start_exchange(nx, gx, gy, outgoing, incoming, es, er)

    order = voxel_order(False)
    cells = [(x, y) for x in range(-1, width_x + 1) for y in range(-1, width_y + 1)]
    own = [(x, y) for x, y in cells if 0 <= x < width_x and 0 <= y < width_y]
    beside = [(x, y) for x, y in cells if 0 <= x < width_x and not 0 <= y < width_y]
    outer_rows = [(x, y) for x, y in cells if not 0 <= x < width_x]

    def place(refs, chosen):
        for first in range(0, len(chosen), 2):
            pair = []
            for x, y in chosen[first : first + 2]:
                ref, at = ext_source(width_x, width_y, refs, x, y)
                pair.append(ref[at])
            both = dot(order, jnp.concatenate(pair, 1), ((1,), (0,))).astype(BF16)
            for j, (x, y) in enumerate(chosen[first : first + 2]):
                column = both[:, j * 128 : (j + 1) * 128]
                i = (x + 1) * wide + y + 1
                ext[i] = column
                ext_t[i] = column.T

    refs = (features, hx, hy, hc)
    place(refs, own)
    partial[...] = jnp.zeros_like(partial)
    finish_exchange(nx, gx, gy, outgoing, incoming, es, er)
    for p in range(bricks):
        rank = send_rank[p]
        returned[pl.ds(p * 64, 64)] = incoming[rank // share, rank % share]

    def spread(g, _):
        rows = pl.ds(pl.multiple_of(g * 256, 256), 256)
        hidden_grad[rows] = dot(returned[rows], w_down[...], ((1,), (1,)))
        return 0

    lax.fori_loop(0, bricks // 4, spread, 0)
    finish_halo(nx, ny, gx, gy, features, halo, hs, hr, ALONG_Y)
    place(refs, beside)

    def windows(p):
        x, y = p // width_y, p % width_y
        return x, y, [(x + 1 + dx) * wide + y + 1 + dy for dx, dy in NEIGHBOURS]

    def forward(p):
        x, y, at = windows(p)
        rows = pl.ds(pl.multiple_of(p * 64, 64), 64)
        present = occupancy[p].astype(F32)
        for k in range(9):
            code = offsets[p * 9 + k]
            chosen = w_sub[jnp.minimum(code, 26)]
            weights[pl.ds(k * 128, 128)] = jnp.where(code < 27, chosen, jnp.zeros_like(chosen))
        window = jnp.concatenate([ext[i] for i in at], 1)
        preact[...] = dot(window, weights[...], ((1,), (0,)))
        for s in range(8):
            part = pl.ds(s * 64, 64)
            lanes = pl.ds(s * 128, 128)
            pre = preact[part]
            sig = jax.nn.sigmoid(pre)
            centre = ext[at[4], part].astype(F32)
            patches[rows, lanes] = (present * (centre + pre * sig)).astype(BF16)
            slope = sig * (1.0 + pre * (1.0 - sig))
            pre_grad[x, y, part] = (present * hidden_grad[rows, lanes] * slope).astype(BF16)

    def kernel_grad(p):
        x, y, at = windows(p)
        window_t = jnp.concatenate([ext_t[i] for i in at], 0)
        outer = dot(window_t, pre_grad[x, y], ((1,), (0,)))
        for k in range(9):
            code = offsets[p * 9 + k]
            term = outer[k * 128 : (k + 1) * 128]
            for o in range(3 * k, 3 * k + 3):
                here = pl.ds(o * 128, 128)
                partial[here] = partial[here] + jnp.where(code == o, term, jnp.zeros_like(term))

    def inner_step(i, _):
        forward(i + width_y)
        kernel_grad(i + width_y)
        return 0

    middle = bricks - 2 * width_y
    lax.fori_loop(0, middle, inner_step, 0)
    finish_halo(nx, ny, gx, gy, features, halo, hs, hr, ALONG_X)
    start_corners(ny, gx, gy, halo, hs, hr)
    ahead = [(x, y) for x, y in outer_rows if 0 <= y < width_y]
    corners = [(x, y) for x, y in outer_rows if not 0 <= y < width_y]
    place(refs, ahead)
    inside = width_y - 2
    jump = (width_x - 1) * width_y

    def rim_inside(i, _):
        forward(i // inside * jump + 1 + i % inside)
        return 0

    lax.fori_loop(0, 2 * inside, rim_inside, 0)
    finish_corners(ny, gx, gy, halo, hs, hr)
    place(refs, corners)
    for side in range(2):

        def rim_ends(i, _, side=side):
            forward(side * jump + i * (width_y - 1))
            return 0

        lax.fori_loop(0, 2, rim_ends, 0)
        start_halo(nx, ny, gx, gy, pre_grad, grad_halo, ps, pr, ALONG_X[side : side + 1])
    start_halo(nx, ny, gx, gy, pre_grad, grad_halo, ps, pr, ALONG_Y)

    def rim(i):
        return i + (i // width_y) * middle

    down = dot(patches[...], w_down[...], ((1,), (0,))).astype(BF16)
    for p in range(bricks):
        shifted[p] = down[p * 64 : (p + 1) * 64]
    for i in range(bricks):
        leaving[i // share, i % share] = shifted[send_order[i]]
    start_exchange(nx, gx, gy, leaving, arrived, ms, mr)

    def rim_grad(i, _):
        kernel_grad(rim(i))
        return 0

    lax.fori_loop(0, 2 * width_y, rim_grad, 0)
    top = 27 * 128
    for s in range(8):
        grad = dot(patches[:, s * 128 : (s + 1) * 128], returned[...], ((0,), (0,)))
        for half in range(2):
            partial[pl.ds(top + half * 1024 + s * 128, 128)] = grad[:, half * 128 : half * 128 + 128]

    back = voxel_order(True)
    grad_refs = (pre_grad, gx_halo, gy_halo, gc_halo)

    def lay(chosen):
        for x, y in chosen:
            ref, at = ext_source(width_x, width_y, grad_refs, x, y)
            ext[(x + 1) * wide + y + 1] = ref[at]

    def column(p):
        x, y, at = windows(p)
        for k in range(9):
            code = offsets[p * 9 + k]
            chosen = w_sub[jnp.maximum(26 - code, 0)]
            back_weights[:, k * 128 : (k + 1) * 128] = jnp.where(
                code < 27, chosen, jnp.zeros_like(chosen)
            )
        window = jnp.concatenate([ext[i] for i in at], 1)
        conv = dot(window, back_weights[...], ((1,), (1,)))
        rows = pl.ds(pl.multiple_of(p * 64, 64), 64)
        spread_rows = jnp.concatenate(
            [hidden_grad[rows, s * 128 : (s + 1) * 128] for s in range(8)], 0
        )
        return (occupancy[p].astype(F32) * (spread_rows + conv)).astype(BF16)

    def pair(i, _):
        p = i * 2
        both = jnp.concatenate([column(p), column(p + 1)], 1)
        out = dot(back, both, ((1,), (0,))).astype(BF16)
        feature_grad[p // width_y, p % width_y] = out[:, :128]
        feature_grad[(p + 1) // width_y, (p + 1) % width_y] = out[:, 128:]
        return 0

    per_row = width_y // 2
    last = bricks // 2
    half = last // 2

    def fill(phase, stage):
        if phase == "scatter" and stage == 0:
            lay(own)
            finish_halo(nx, ny, gx, gy, pre_grad, grad_halo, ps, pr, ALONG_Y)
            lay(beside)
        if phase == "scatter" and stage == 1:
            lax.fori_loop(per_row, last - per_row, pair, 0)
        if phase == "gather" and stage == stages - 1:
            finish_halo(nx, ny, gx, gy, pre_grad, grad_halo, ps, pr, ALONG_X)
            start_corners(ny, gx, gy, grad_halo, ps, pr)
            lay(ahead)
        if phase == "gather" and stage == stages - 2:
            finish_corners(ny, gx, gy, grad_halo, ps, pr)
            lay(corners)

            def rim_pair(i, _):
                return pair(i + (i // per_row) * (last - 2 * per_row), 0)

            lax.fori_loop(0, 2 * per_row, rim_pair, 0)
        if phase == "gather" and stage == 0:
            finish_exchange(nx, gx, gy, leaving, arrived, ms, mr)
            for p in range(bricks):
                rank = cell_rank[p]
                coarse[p // width_y, p % width_y] = arrived[rank // share, rank % share]

    reduce_all(nx, ny, gx, gy, partial, total, sends, recvs, ss, rs, gs, gr, fill)


def ranks(keys):
    rank = jnp.sum((keys[None, :] < keys[:, None]).astype(jnp.int32), 1)
    places = jnp.arange(keys.shape[0], dtype=jnp.int32)
    order = jnp.sum((rank[None, :] == places[:, None]).astype(jnp.int32) * places[None, :], 1)
    return rank, order


def local(nx, ny, features, occupancy, pair_offset, owner, w_sub, w_down, cotangent):
    width_x, width_y, voxels, channels = features.shape
    bricks = width_x * width_y
    cells, out_channels = cotangent.shape[2:]
    share = bricks // nx
    occupied = occupancy.reshape(bricks)
    offsets = pair_offset.reshape(bricks * 9)
    targets = owner.reshape(bricks)
    places = jnp.arange(bricks, dtype=jnp.int32)
    source = (2 * lax.axis_index("gx") - targets + nx) % nx
    send_rank, send_order = ranks(targets * bricks + places)
    cell_rank, cell_order = ranks(source * bricks + places)

    vmem = pl.BlockSpec(memory_space=pltpu.VMEM)
    smem = pl.BlockSpec(memory_space=pltpu.SMEM)
    shape = jax.ShapeDtypeStruct
    dma = pltpu.SemaphoreType.DMA
    halo_buffers = [
        pltpu.VMEM((2, width_y, voxels, channels), BF16),
        pltpu.VMEM((2, width_x, voxels, channels), BF16),
        pltpu.VMEM((4, voxels, channels), BF16),
    ]
    block = pltpu.VMEM((nx, share, cells, out_channels), BF16)
    unit = 16 * nx * ny
    rows = -(-(27 * channels + 2048) // unit) * unit
    stages = len(groups(nx, ny))
    buffers = []
    count = 0
    for _, length, plan in pieces(nx, ny, rows):
        for _, _, size in plan:
            length //= size
            buffers.append(pltpu.VMEM((size - 1, length, 128), BF16))
            count += size - 1
    around = (width_x + 2) * (width_y + 2)
    coarse, feature_grad, total = pl.pallas_call(
        functools.partial(whole_kernel, nx, ny, stages),
        out_shape=[
            shape(cotangent.shape, BF16),
            shape(features.shape, BF16),
            shape((rows, 128), BF16),
        ],
        in_specs=[smem] * 6 + [vmem] * 4,
        out_specs=[vmem] * 3,
        scratch_shapes=buffers
        + buffers
        + halo_buffers
        + halo_buffers
        + [block] * 4
        + [
            pltpu.VMEM(features.shape, BF16),
            pltpu.VMEM((around, voxels, channels), BF16),
            pltpu.VMEM((around, channels, voxels), BF16),
            pltpu.VMEM((9 * channels, channels), BF16),
            pltpu.VMEM((channels, 9 * channels), BF16),
            pltpu.VMEM((voxels, channels), F32),
            pltpu.VMEM((bricks * cells, 8 * channels), BF16),
            pltpu.VMEM((bricks * cells, 8 * channels), F32),
            pltpu.VMEM((bricks * cells, out_channels), BF16),
            pltpu.VMEM((bricks, cells, out_channels), BF16),
            pltpu.VMEM((rows, 128), F32),
        ]
        + [dma((9,)), dma((9,)), dma((nx,)), dma((nx,))] * 2
        + [dma((count,))] * 4,
        compiler_params=pltpu.CompilerParams(
            collective_id=0, has_side_effects=True, vmem_limit_bytes=VMEM_LIMIT
        ),
        name="section",
    )(
        occupied,
        offsets,
        send_rank,
        send_order,
        cell_rank,
        cell_order,
        features,
        cotangent.reshape(bricks, cells, out_channels),
        w_sub,
        w_down,
    )
    scale = 1.0 / (nx * ny)
    top = 27 * channels
    sides = total[top : top + 2048].reshape(2, 1024, 128)
    sub_grad = total[:top].astype(F32).reshape(w_sub.shape) * scale
    down_grad = jnp.concatenate([sides[0], sides[1]], 1).astype(F32) * scale
    return coarse, feature_grad, sub_grad, down_grad


def solution(mesh):
    in_specs = (
        P("gx", "gy", None, None),
        P("gx", "gy"),
        P("gx", "gy", None),
        P("gx", "gy"),
        P(),
        P(),
        P("gx", "gy", None, None),
    )
    out_specs = (P("gx", "gy", None, None), P("gx", "gy", None, None), P(), P())
    return jax.shard_map(
        functools.partial(local, mesh.shape["gx"], mesh.shape["gy"]),
        mesh=mesh,
        in_specs=in_specs,
        out_specs=out_specs,
        check_vma=False,
    )
```

```python
import functools

import jax
import jax.numpy as jnp
from jax import lax
from jax.experimental import pallas as pl
from jax.experimental.pallas import tpu as pltpu
from jax.sharding import PartitionSpec as P

MESH = pl.DeviceIdType.MESH
E = 8
NEIGHBOURS = [(-1, -1), (-1, 0), (-1, 1), (0, -1), (0, 0), (0, 1), (1, -1), (1, 0), (1, 1)]
ALONG_X = [1, 7]
ALONG_Y = [3, 5]
HALO = ALONG_X + ALONG_Y
F32 = jnp.float32
BF16 = jnp.bfloat16
VMEM_LIMIT = 58 * 1024 * 1024


def position():
    return lax.axis_index("gx"), lax.axis_index("gy")


def exists(nx, ny, gx, gy, k):
    dx, dy = NEIGHBOURS[k]
    x, y = gx + dx, gy + dy
    return (x >= 0) & (x < nx) & (y >= 0) & (y < ny)


def edge(ref, width_x, width_y, k):
    dx, dy = NEIGHBOURS[k]
    sx = {-1: 0, 0: slice(None), 1: width_x - 1}[dx]
    sy = {-1: 0, 0: slice(None), 1: width_y - 1}[dy]
    return ref.at[sx, sy]


def slot(halo, k):
    hx, hy, hc = halo
    dx, dy = NEIGHBOURS[k]
    if dy == 0:
        return hx.at[(dx + 1) // 2]
    if dx == 0:
        return hy.at[(dy + 1) // 2]
    return hc.at[(dx + 1) // 2 * 2 + (dy + 1) // 2]


def halo_copy(nx, ny, gx, gy, source, halo, send, recv, k):
    dx, dy = NEIGHBOURS[k]
    return pltpu.make_async_remote_copy(
        src_ref=edge(source, source.shape[0], source.shape[1], k),
        dst_ref=slot(halo, 8 - k),
        send_sem=send.at[k],
        recv_sem=recv.at[8 - k],
        device_id=(gx + dx, gy + dy),
        device_id_type=MESH,
    )


def halo_arrival(nx, ny, gx, gy, source, halo, send, recv, k):
    dx, dy = NEIGHBOURS[k]
    return pltpu.make_async_remote_copy(
        src_ref=edge(source, source.shape[0], source.shape[1], 8 - k),
        dst_ref=slot(halo, k),
        send_sem=send.at[8 - k],
        recv_sem=recv.at[k],
        device_id=(gx + dx, gy + dy),
        device_id_type=MESH,
    )


def halo_fill(source, halo, recv, k):
    return pltpu.make_async_copy(
        edge(source, source.shape[0], source.shape[1], k), slot(halo, k), recv.at[k]
    )


def start_halo(nx, ny, gx, gy, source, halo, send, recv, chosen):
    for k in chosen:
        there = exists(nx, ny, gx, gy, k)

        @pl.when(there)
        def _(k=k):
            halo_copy(nx, ny, gx, gy, source, halo, send, recv, k).start()

        @pl.when(jnp.logical_not(there))
        def _(k=k):
            halo_fill(source, halo, recv, k).start()


def finish_halo(nx, ny, gx, gy, source, halo, send, recv, chosen):
    for k in chosen:
        there = exists(nx, ny, gx, gy, k)

        @pl.when(there)
        def _(k=k):
            halo_copy(nx, ny, gx, gy, source, halo, send, recv, k).wait_send()
            halo_arrival(nx, ny, gx, gy, source, halo, send, recv, k).wait_recv()

        @pl.when(jnp.logical_not(there))
        def _(k=k):
            halo_fill(source, halo, recv, k).wait()


def corner_copy(gx, gy, halo, send, recv, side, dy):
    hx, _, hc = halo
    dx = 2 * side - 1
    column = 0 if dy < 0 else hx.shape[1] - 1
    here, there = 3 * (dx + 1) + dy + 1, 3 * (dx + 1) - dy + 1
    return pltpu.make_async_remote_copy(
        src_ref=hx.at[side, column],
        dst_ref=hc.at[2 * side + (1 - dy) // 2],
        send_sem=send.at[here],
        recv_sem=recv.at[there],
        device_id=(gx, gy + dy),
        device_id_type=MESH,
    )


def corner_arrival(gx, gy, halo, send, recv, side, dy):
    hx, _, hc = halo
    k = 3 * 2 * side + dy + 1
    return pltpu.make_async_remote_copy(
        src_ref=hx.at[side, 0],
        dst_ref=hc.at[2 * side + (1 + dy) // 2],
        send_sem=send.at[k],
        recv_sem=recv.at[k],
        device_id=(gx, gy + dy),
        device_id_type=MESH,
    )


def corner_fill(halo, recv, side, dy):
    hx, _, hc = halo
    return pltpu.make_async_copy(
        hx.at[side, 0], hc.at[2 * side + (1 + dy) // 2], recv.at[3 * 2 * side + dy + 1]
    )


def start_corners(ny, gx, gy, halo, send, recv):
    for side in range(2):
        for dy in (-1, 1):
            there = (gy + dy >= 0) & (gy + dy < ny)

            @pl.when(there)
            def _(side=side, dy=dy):
                corner_copy(gx, gy, halo, send, recv, side, dy).start()

            @pl.when(jnp.logical_not(there))
            def _(side=side, dy=dy):
                corner_fill(halo, recv, side, dy).start()


def finish_corners(ny, gx, gy, halo, send, recv):
    for side in range(2):
        for dy in (-1, 1):
            there = (gy + dy >= 0) & (gy + dy < ny)

            @pl.when(there)
            def _(side=side, dy=dy):
                corner_copy(gx, gy, halo, send, recv, side, dy).wait_send()
                corner_arrival(gx, gy, halo, send, recv, side, dy).wait_recv()

            @pl.when(jnp.logical_not(there))
            def _(side=side, dy=dy):
                corner_fill(halo, recv, side, dy).wait()


def exchange_copy(nx, gx, gy, outgoing, incoming, send, recv, shift):
    peer = lax.rem(gx + shift, nx)
    return pltpu.make_async_remote_copy(
        src_ref=outgoing.at[peer],
        dst_ref=incoming.at[gx],
        send_sem=send.at[shift],
        recv_sem=recv.at[shift],
        device_id=(peer, gy),
        device_id_type=MESH,
    )


def exchange_arrival(nx, gx, gy, outgoing, incoming, send, recv, shift):
    peer = lax.rem(gx + nx - shift, nx)
    return pltpu.make_async_remote_copy(
        src_ref=outgoing.at[peer],
        dst_ref=incoming.at[peer],
        send_sem=send.at[shift],
        recv_sem=recv.at[shift],
        device_id=(peer, gy),
        device_id_type=MESH,
    )


def start_exchange(nx, gx, gy, outgoing, incoming, send, recv):
    pltpu.make_async_copy(outgoing.at[gx], incoming.at[gx], recv.at[0]).start()
    for shift in range(1, nx):
        exchange_copy(nx, gx, gy, outgoing, incoming, send, recv, shift).start()


def finish_exchange(nx, gx, gy, outgoing, incoming, send, recv):
    pltpu.make_async_copy(outgoing.at[gx], incoming.at[gx], recv.at[0]).wait()
    for shift in range(1, nx):
        exchange_copy(nx, gx, gy, outgoing, incoming, send, recv, shift).wait_send()
        exchange_arrival(nx, gx, gy, outgoing, incoming, send, recv, shift).wait_recv()


def greet(nx, ny, gx, gy, partners):
    barrier = pltpu.get_barrier_semaphore()
    for k in HALO:
        dx, dy = NEIGHBOURS[k]

        @pl.when(exists(nx, ny, gx, gy, k))
        def _(dx=dx, dy=dy):
            pl.semaphore_signal(
                barrier, inc=1, device_id=(gx + dx, gy + dy), device_id_type=MESH
            )

    for shift in range(1, nx):
        pl.semaphore_signal(
            barrier, inc=1, device_id=(lax.rem(gx + shift, nx), gy), device_id_type=MESH
        )
    for partner in partners:
        pl.semaphore_signal(barrier, inc=1, device_id=partner, device_id_type=MESH)
    count = nx - 1 + len(partners)
    for k in HALO:
        count = count + jnp.where(exists(nx, ny, gx, gy, k), 1, 0)
    pl.semaphore_wait(barrier, count)


def groups(nx, ny):
    deep = 4 if nx % 4 == 0 else 1
    return [
        (axis, stride, size)
        for axis, stride, size in (
            (1, 1, 2),
            (1, 2, ny // 2),
            (0, 1, nx // deep),
            (0, nx // deep, deep),
        )
        if size > 1
    ]


def member(gx, gy, group, shift):
    axis, stride, size = group
    here = (gx, gy)[axis]
    own = lax.rem(lax.div(here, stride), size)
    other = lax.rem(own + shift, size)
    there = here + (other - own) * stride
    return own, other, ((there, gy) if axis == 0 else (gx, there))


def pieces(nx, ny, rows):
    plan = groups(nx, ny)
    unit = 16 * nx * ny
    first = rows // unit // 2 * unit
    turned = plan[:1] + plan[1:-1][::-1] + plan[-1:]
    return [(0, first, plan), (first, rows - first, turned)]


def reduce_all(nx, ny, gx, gy, partial, total, sends, recvs, ss, rs, gs, gr, fill):
    work = pieces(nx, ny, partial.shape[0])
    stages = len(work[0][2])
    base = [start for start, _, _ in work]
    length = [count for _, count, _ in work]
    bases = [[] for _ in work]
    sem = 0
    for stage in range(stages):
        copies = []
        for w, (_, _, plan) in enumerate(work):
            group = plan[stage]
            size = group[2]
            chunk = length[w] // size
            buffer = w * stages + stage
            for shift in range(1, size):
                own, other, device = member(gx, gy, group, shift)
                start = pl.multiple_of(base[w] + other * chunk, 16)
                sends[buffer][shift - 1] = partial[pl.ds(start, chunk)].astype(BF16)
                copy = pltpu.make_async_remote_copy(
                    src_ref=sends[buffer].at[shift - 1],
                    dst_ref=recvs[buffer].at[shift - 1],
                    send_sem=ss.at[sem],
                    recv_sem=rs.at[sem],
                    device_id=device,
                    device_id_type=MESH,
                )
                copy.start()
                copies.append(copy)
                sem += 1
            bases[w].append(base[w])
            base[w] = pl.multiple_of(base[w] + own * chunk, 16)
            length[w] = chunk
        fill("scatter", stage)
        for copy in copies:
            copy.wait()
        for w, (_, _, plan) in enumerate(work):
            buffer = w * stages + stage
            here = pl.ds(base[w], length[w])
            value = partial[here]
            for shift in range(1, plan[stage][2]):
                value = value + recvs[buffer][shift - 1].astype(F32)
            partial[here] = value
    for w in range(len(work)):
        here = pl.ds(base[w], length[w])
        total[here] = partial[here].astype(BF16)
    sem = 0
    for stage in reversed(range(stages)):
        copies = []
        for w, (_, _, plan) in enumerate(work):
            group = plan[stage]
            size = group[2]
            here = pl.ds(base[w], length[w])
            for shift in range(1, size):
                own, other, device = member(gx, gy, group, shift)
                back = lax.rem(own + size - shift, size)
                landing = pl.multiple_of(bases[w][stage] + back * length[w], 16)
                copy = pltpu.make_async_remote_copy(
                    src_ref=total.at[here],
                    dst_ref=total.at[here],
                    send_sem=gs.at[sem],
                    recv_sem=gr.at[sem],
                    device_id=device,
                    device_id_type=MESH,
                )
                copy.start()
                arrival = pltpu.make_async_remote_copy(
                    src_ref=total.at[here],
                    dst_ref=total.at[pl.ds(landing, length[w])],
                    send_sem=gs.at[sem],
                    recv_sem=gr.at[sem],
                    device_id=device,
                    device_id_type=MESH,
                )
                copies.append((copy, arrival))
                sem += 1
        fill("gather", stage)
        for copy, arrival in copies:
            copy.wait_send()
            arrival.wait_recv()
        for w, (_, _, plan) in enumerate(work):
            base[w] = bases[w][stage]
            length[w] = length[w] * plan[stage][2]


def ext_source(width_x, width_y, refs, x, y):
    own, hx, hy, hc = refs
    sx = 0 if x < 0 else (2 if x >= width_x else 1)
    sy = 0 if y < 0 else (2 if y >= width_y else 1)
    if sx == 1 and sy == 1:
        return own, (x, y)
    if sy == 1:
        return hx, (sx // 2, y)
    if sx == 1:
        return hy, (sy // 2, x)
    return hc, (sx // 2 * 2 + sy // 2,)


def voxel_order(transposed):
    row = lax.broadcasted_iota(jnp.int32, (E**3, E**3), 1 if transposed else 0)
    column = lax.broadcasted_iota(jnp.int32, (E**3, E**3), 0 if transposed else 1)
    sub, cell = row // 64, row % 64
    a = (cell // 16) * 2 + sub // 4
    b = (cell // 4) % 4 * 2 + (sub // 2) % 2
    c = cell % 4 * 2 + sub % 2
    return jnp.where(column == (a * 8 + b) * 8 + c, 1.0, 0.0).astype(BF16)


def dot(a, b, dims):
    return lax.dot_general(a, b, (dims, ((), ())), preferred_element_type=F32)


def whole_kernel(
    nx,
    ny,
    stages,
    occupancy,
    offsets,
    send_rank,
    send_order,
    cell_rank,
    cell_order,
    features,
    cotangent,
    w_sub,
    w_down,
    coarse,
    feature_grad,
    total,
    *scratch,
):
    buffers = 2 * stages
    sends, recvs = scratch[:buffers], scratch[buffers : 2 * buffers]
    (
        hx, hy, hc, gx_halo, gy_halo, gc_halo,
        outgoing, incoming, leaving, arrived,
        pre_grad, ext, ext_t, weights, back_weights, preact, patches, hidden_grad, slopes,
        returned, shifted, partial,
        hs, hr, es, er, ps, pr, ms, mr, ss, rs, gs, gr,
    ) = scratch[2 * buffers :]
    width_x, width_y = features.shape[:2]
    bricks = width_x * width_y
    wide = width_y + 2
    share = outgoing.shape[1]
    gx, gy = position()
    halo = (hx, hy, hc)
    grad_halo = (gx_halo, gy_halo, gc_halo)
    plan = groups(nx, ny)
    partners = [
        member(gx, gy, group, shift)[2] for group in plan for shift in range(1, group[2])
    ]
    greet(nx, ny, gx, gy, partners)
    start_halo(nx, ny, gx, gy, features, halo, hs, hr, HALO)
    for i in range(bricks):
        outgoing[i // share, i % share] = cotangent[cell_order[i]]

    order = voxel_order(False)
    cells = [(x, y) for x in range(-1, width_x + 1) for y in range(-1, width_y + 1)]
    own = [(x, y) for x, y in cells if 0 <= x < width_x and 0 <= y < width_y]
    beside = [(x, y) for x, y in cells if 0 <= x < width_x and not 0 <= y < width_y]
    outer_rows = [(x, y) for x, y in cells if not 0 <= x < width_x]

    def place(refs, chosen):
        for first in range(0, len(chosen), 2):
            pair = []
            for x, y in chosen[first : first + 2]:
                ref, at = ext_source(width_x, width_y, refs, x, y)
                pair.append(ref[at])
            both = dot(order, jnp.concatenate(pair, 1), ((1,), (0,))).astype(BF16)
            for j, (x, y) in enumerate(chosen[first : first + 2]):
                column = both[:, j * 128 : (j + 1) * 128]
                i = (x + 1) * wide + y + 1
                ext[i] = column
                ext_t[i] = column.T

    refs = (features, hx, hy, hc)
    place(refs, own)
    partial[...] = jnp.zeros_like(partial)
    finish_halo(nx, ny, gx, gy, features, halo, hs, hr, ALONG_Y)
    place(refs, beside)

    def windows(p):
        x, y = p // width_y, p % width_y
        return x, y, [(x + 1 + dx) * wide + y + 1 + dy for dx, dy in NEIGHBOURS]

    def forward(p):
        x, y, at = windows(p)
        rows = pl.ds(pl.multiple_of(p * 64, 64), 64)
        present = occupancy[p].astype(F32)
        for k in range(9):
            code = offsets[p * 9 + k]
            chosen = w_sub[jnp.minimum(code, 26)]
            weights[pl.ds(k * 128, 128)] = jnp.where(code < 27, chosen, jnp.zeros_like(chosen))
        window = jnp.concatenate([ext[i] for i in at], 1)
        preact[...] = dot(window, weights[...], ((1,), (0,)))
        for s in range(8):
            part = pl.ds(s * 64, 64)
            lanes = pl.ds(s * 128, 128)
            pre = preact[part]
            sig = jax.nn.sigmoid(pre)
            centre = ext[at[4], part].astype(F32)
            patches[rows, lanes] = (present * (centre + pre * sig)).astype(BF16)
            slope = sig * (1.0 + pre * (1.0 - sig))
            slopes[p, part] = slope

    def gradient(p, _):
        x, y = p // width_y, p % width_y
        rows = pl.ds(pl.multiple_of(p * 64, 64), 64)
        present = occupancy[p].astype(F32)
        for s in range(8):
            part = pl.ds(s * 64, 64)
            grad = present * hidden_grad[rows, s * 128 : (s + 1) * 128] * slopes[p, part]
            pre_grad[x, y, part] = grad.astype(BF16)
        return 0

    def kernel_grad(p):
        x, y, at = windows(p)
        window_t = jnp.concatenate([ext_t[i] for i in at], 0)
        outer = dot(window_t, pre_grad[x, y], ((1,), (0,)))
        for k in range(9):
            code = offsets[p * 9 + k]
            term = outer[k * 128 : (k + 1) * 128]
            for o in range(3 * k, 3 * k + 3):
                here = pl.ds(o * 128, 128)
                partial[here] = partial[here] + jnp.where(code == o, term, jnp.zeros_like(term))

    def inner_step(i, _):
        forward(i + width_y)
        return 0

    middle = bricks - 2 * width_y
    lax.fori_loop(0, middle, inner_step, 0)
    finish_halo(nx, ny, gx, gy, features, halo, hs, hr, ALONG_X)
    start_corners(ny, gx, gy, halo, hs, hr)
    start_exchange(nx, gx, gy, outgoing, incoming, es, er)
    ahead = [(x, y) for x, y in outer_rows if 0 <= y < width_y]
    corners = [(x, y) for x, y in outer_rows if not 0 <= y < width_y]
    place(refs, ahead)
    inside = width_y - 2
    jump = (width_x - 1) * width_y

    def rim_inside(i, _):
        forward(i // inside * jump + 1 + i % inside)
        return 0

    lax.fori_loop(0, 2 * inside, rim_inside, 0)
    finish_corners(ny, gx, gy, halo, hs, hr)
    place(refs, corners)
    for side in range(2):

        def rim_ends(i, _, side=side):
            forward(side * jump + i * (width_y - 1))
            return 0

        lax.fori_loop(0, 2, rim_ends, 0)

    down = dot(patches[...], w_down[...], ((1,), (0,))).astype(BF16)
    for p in range(bricks):
        shifted[p] = down[p * 64 : (p + 1) * 64]
    for i in range(bricks):
        leaving[i // share, i % share] = shifted[send_order[i]]
    finish_exchange(nx, gx, gy, outgoing, incoming, es, er)
    for p in range(bricks):
        rank = send_rank[p]
        returned[pl.ds(p * 64, 64)] = incoming[rank // share, rank % share]

    def spread(g, _):
        rows = pl.ds(pl.multiple_of(g * 256, 256), 256)
        hidden_grad[rows] = dot(returned[rows], w_down[...], ((1,), (1,)))
        return 0

    lax.fori_loop(0, bricks // 4, spread, 0)
    for side in range(2):
        lax.fori_loop(side * jump, side * jump + width_y, gradient, 0)
        start_halo(nx, ny, gx, gy, pre_grad, grad_halo, ps, pr, ALONG_X[side : side + 1])
    lax.fori_loop(width_y, bricks - width_y, gradient, 0)
    start_halo(nx, ny, gx, gy, pre_grad, grad_halo, ps, pr, ALONG_Y)

    def every_grad(p, _):
        kernel_grad(p)
        return 0

    lax.fori_loop(0, bricks, every_grad, 0)
    top = 27 * 128
    for s in range(8):
        grad = dot(patches[:, s * 128 : (s + 1) * 128], returned[...], ((0,), (0,)))
        for half in range(2):
            partial[pl.ds(top + half * 1024 + s * 128, 128)] = grad[:, half * 128 : half * 128 + 128]

    back = voxel_order(True)
    grad_refs = (pre_grad, gx_halo, gy_halo, gc_halo)

    def lay(chosen):
        for x, y in chosen:
            ref, at = ext_source(width_x, width_y, grad_refs, x, y)
            ext[(x + 1) * wide + y + 1] = ref[at]

    def column(p):
        x, y, at = windows(p)
        for k in range(9):
            code = offsets[p * 9 + k]
            chosen = w_sub[jnp.maximum(26 - code, 0)]
            back_weights[:, k * 128 : (k + 1) * 128] = jnp.where(
                code < 27, chosen, jnp.zeros_like(chosen)
            )
        window = jnp.concatenate([ext[i] for i in at], 1)
        conv = dot(window, back_weights[...], ((1,), (1,)))
        rows = pl.ds(pl.multiple_of(p * 64, 64), 64)
        spread_rows = jnp.concatenate(
            [hidden_grad[rows, s * 128 : (s + 1) * 128] for s in range(8)], 0
        )
        return (occupancy[p].astype(F32) * (spread_rows + conv)).astype(BF16)

    def pair(i, _):
        p = i * 2
        both = jnp.concatenate([column(p), column(p + 1)], 1)
        out = dot(back, both, ((1,), (0,))).astype(BF16)
        feature_grad[p // width_y, p % width_y] = out[:, :128]
        feature_grad[(p + 1) // width_y, (p + 1) % width_y] = out[:, 128:]
        return 0

    per_row = width_y // 2
    last = bricks // 2
    half = last // 2

    def fill(phase, stage):
        if phase == "scatter" and stage == 0:
            lay(own)
            finish_halo(nx, ny, gx, gy, pre_grad, grad_halo, ps, pr, ALONG_Y)
            lay(beside)
        if phase == "scatter" and stage == 1:
            lax.fori_loop(per_row, last - per_row, pair, 0)
        if phase == "gather" and stage == stages - 1:
            finish_halo(nx, ny, gx, gy, pre_grad, grad_halo, ps, pr, ALONG_X)
            start_corners(ny, gx, gy, grad_halo, ps, pr)
            start_exchange(nx, gx, gy, leaving, arrived, ms, mr)
            lay(ahead)
        if phase == "gather" and stage == stages - 2:
            finish_corners(ny, gx, gy, grad_halo, ps, pr)
            lay(corners)

            def rim_pair(i, _):
                return pair(i + (i // per_row) * (last - 2 * per_row), 0)

            lax.fori_loop(0, 2 * per_row, rim_pair, 0)
        if phase == "gather" and stage == 0:
            finish_exchange(nx, gx, gy, leaving, arrived, ms, mr)
            for p in range(bricks):
                rank = cell_rank[p]
                coarse[p // width_y, p % width_y] = arrived[rank // share, rank % share]

    reduce_all(nx, ny, gx, gy, partial, total, sends, recvs, ss, rs, gs, gr, fill)


def ranks(keys):
    rank = jnp.sum((keys[None, :] < keys[:, None]).astype(jnp.int32), 1)
    places = jnp.arange(keys.shape[0], dtype=jnp.int32)
    order = jnp.sum((rank[None, :] == places[:, None]).astype(jnp.int32) * places[None, :], 1)
    return rank, order


def local(nx, ny, features, occupancy, pair_offset, owner, w_sub, w_down, cotangent):
    width_x, width_y, voxels, channels = features.shape
    bricks = width_x * width_y
    cells, out_channels = cotangent.shape[2:]
    share = bricks // nx
    occupied = occupancy.reshape(bricks)
    offsets = pair_offset.reshape(bricks * 9)
    targets = owner.reshape(bricks)
    places = jnp.arange(bricks, dtype=jnp.int32)
    source = (2 * lax.axis_index("gx") - targets + nx) % nx
    send_rank, send_order = ranks(targets * bricks + places)
    cell_rank, cell_order = ranks(source * bricks + places)

    vmem = pl.BlockSpec(memory_space=pltpu.VMEM)
    smem = pl.BlockSpec(memory_space=pltpu.SMEM)
    shape = jax.ShapeDtypeStruct
    dma = pltpu.SemaphoreType.DMA
    halo_buffers = [
        pltpu.VMEM((2, width_y, voxels, channels), BF16),
        pltpu.VMEM((2, width_x, voxels, channels), BF16),
        pltpu.VMEM((4, voxels, channels), BF16),
    ]
    block = pltpu.VMEM((nx, share, cells, out_channels), BF16)
    unit = 16 * nx * ny
    rows = -(-(27 * channels + 2048) // unit) * unit
    stages = len(groups(nx, ny))
    buffers = []
    count = 0
    for _, length, plan in pieces(nx, ny, rows):
        for _, _, size in plan:
            length //= size
            buffers.append(pltpu.VMEM((size - 1, length, 128), BF16))
            count += size - 1
    around = (width_x + 2) * (width_y + 2)
    coarse, feature_grad, total = pl.pallas_call(
        functools.partial(whole_kernel, nx, ny, stages),
        out_shape=[
            shape(cotangent.shape, BF16),
            shape(features.shape, BF16),
            shape((rows, 128), BF16),
        ],
        in_specs=[smem] * 6 + [vmem] * 4,
        out_specs=[vmem] * 3,
        scratch_shapes=buffers
        + buffers
        + halo_buffers
        + halo_buffers
        + [block] * 4
        + [
            pltpu.VMEM(features.shape, BF16),
            pltpu.VMEM((around, voxels, channels), BF16),
            pltpu.VMEM((around, channels, voxels), BF16),
            pltpu.VMEM((9 * channels, channels), BF16),
            pltpu.VMEM((channels, 9 * channels), BF16),
            pltpu.VMEM((voxels, channels), F32),
            pltpu.VMEM((bricks * cells, 8 * channels), BF16),
            pltpu.VMEM((bricks * cells, 8 * channels), F32),
            pltpu.VMEM((bricks, voxels, channels), F32),
            pltpu.VMEM((bricks * cells, out_channels), BF16),
            pltpu.VMEM((bricks, cells, out_channels), BF16),
            pltpu.VMEM((rows, 128), F32),
        ]
        + [dma((9,)), dma((9,)), dma((nx,)), dma((nx,))] * 2
        + [dma((count,))] * 4,
        compiler_params=pltpu.CompilerParams(
            collective_id=0, has_side_effects=True, vmem_limit_bytes=VMEM_LIMIT
        ),
        name="section",
    )(
        occupied,
        offsets,
        send_rank,
        send_order,
        cell_rank,
        cell_order,
        features,
        cotangent.reshape(bricks, cells, out_channels),
        w_sub,
        w_down,
    )
    scale = 1.0 / (nx * ny)
    top = 27 * channels
    sides = total[top : top + 2048].reshape(2, 1024, 128)
    sub_grad = total[:top].astype(F32).reshape(w_sub.shape) * scale
    down_grad = jnp.concatenate([sides[0], sides[1]], 1).astype(F32) * scale
    return coarse, feature_grad, sub_grad, down_grad


def solution(mesh):
    in_specs = (
        P("gx", "gy", None, None),
        P("gx", "gy"),
        P("gx", "gy", None),
        P("gx", "gy"),
        P(),
        P(),
        P("gx", "gy", None, None),
    )
    out_specs = (P("gx", "gy", None, None), P("gx", "gy", None, None), P(), P())
    return jax.shard_map(
        functools.partial(local, mesh.shape["gx"], mesh.shape["gy"]),
        mesh=mesh,
        in_specs=in_specs,
        out_specs=out_specs,
        check_vma=False,
    )
```
